256 devices in a mesh: ed: 32 (over y, z), tp: 8 (over x, core).
Axes of the slice: x: 4, y: 4, z: 8, core: 2. Of those that a mesh axis runs over, the one named last changes fastest.
Arguments:
- tokens: bfloat16 [1024, 6144], P('ed'), may hold values from -6 to 6
- expert_ids: int32 [1024, 2], P('ed'), may hold values from 0 to 3, all different within a row; in each aligned block of 32 rows (0 to 31, 32 to 63, ...) at most 24 rows name the same one
- router_logits: float32 [1024, 4], P('ed'), may hold values from -6 to 6
- gate_weight: bfloat16 [32, 6144, 2048], P('ed', None, 'tp'), may hold values from -0.078125 to 0.078125
- up_weight: bfloat16 [32, 6144, 2048], P('ed', None, 'tp'), may hold values from -0.078125 to 0.078125
- down_weight: bfloat16 [32, 2048, 6144], P('ed', 'tp'), may hold values from -0.046875 to 0.046875
Outputs:
- mixed: bfloat16 [1024, 6144], P('ed', 'tp')
The draws below stay inside these ranges and needn't reach their ends.
Inputs may be any that keep to these rules, and one draw needn't show every extreme that they name: `expert_ids`: each row names two different experts. Among the 32 rows of one device no expert is named by more than 24 rows, and in every draw some expert is named by exactly 24 rows of some device.
All inputs are finite; a program needn't handle non-finite values.
Results may differ from the reference program's by a relative error of at most 0.0049.
Values may be sent and summed in bfloat16 or wider, within the bound.
A program may use at most 128 MiB of HBM per device.

```python
import math
import jax
import jax.numpy as jnp
import numpy as np

D = 6144
FF = 16384
EXPERTS = 4
TOK_DEV = 32
GROUP = 8
MOST = 24
TOKENS = 1024
N_ED = 32


def block_levels(own_key, shape, shards, smallest, top_value):
    factor_of, own = 1.0, jax.random.fold_in(own_key, 6)
    for axis_at, shards_of in shards:
        heights = jnp.exp(jax.random.uniform(jax.random.fold_in(own, axis_at), (shards_of,), jnp.float32, smallest / len(shards), top_value / len(shards)))
        factor_of = factor_of * jnp.repeat(heights, shape[axis_at] // shards_of).reshape([-1 if axis == axis_at else 1 for axis in range(len(shape))])
    return factor_of


def deal_out(key, own, number, rows, number_of, top, bound, skew):
    sequence = jax.random.permutation(key, number_of)
    packed, common = load_shares(number_of, rows * top, bound, skew, True), load_shares(number_of, rows * top, bound, skew, False)
    places = jnp.arange(number_of)

    def named(tallies, offset_by):
        used = int((tallies > 0).sum())
        fixed = max(1, used // 4)
        moved = fixed + (places - fixed + offset_by * (used - fixed)) % max(1, number_of - fixed)
        return jnp.zeros((number_of,), jnp.int32).at[sequence[jnp.where(places < fixed, places, moved)]].set(jnp.asarray(tallies, jnp.int32))

    tallies = jnp.where(number % 4 == 0, named(packed, number // 4), named(common, number - number // 4 - 1))
    mixed = jax.random.permutation(jax.random.fold_in(own, 3), number_of)
    donor, taker = mixed[0:number_of // 2 * 2:2], mixed[1:number_of // 2 * 2:2]
    margin = jnp.minimum(tallies[donor] - 1, bound - tallies[taker]) // 2
    margin = jnp.where((donor == sequence[0]) | (taker == sequence[0]) | (tallies[taker] == 0), 0, jnp.maximum(margin, 0))
    moved = jax.random.randint(jax.random.fold_in(own, 4), (number_of // 2,), 0, 1 << 20) % (margin + 1)
    tallies = tallies.at[donor].add(-moved).at[taker].add(moved)
    labels = jnp.searchsorted(jnp.cumsum(tallies), jnp.arange(rows * top), side="right").astype(jnp.int32)
    listing = labels.reshape(top, rows).T
    listing = listing[jax.random.permutation(jax.random.fold_in(own, 1), rows)]
    offset_by = jax.random.randint(jax.random.fold_in(own, 2), (rows, 1), 0, top)
    return jnp.take_along_axis(listing, (jnp.arange(top)[None, :] + offset_by) % top, axis=1)


def load_shares(count, total, limit, lean, full):
    portions = [(1 << 20) // math.isqrt(standing ** lean) + 1 for standing in range(1, count + 1)]
    largest = limit if full else min(limit, max(-(-total // count), total * portions[0] // sum(portions)))
    least = 1 if total - largest >= count - 1 else 0
    counts, spare = [largest] + [least] * (count - 1), total - largest - least * (count - 1)
    while spare > 0:
        candidates = [i for i in range(1, count) if counts[i] < largest] or [i for i in range(1, count) if counts[i] < limit]
        whole, left = sum([portions[i] for i in candidates]), spare
        for i in candidates:
            addition = min(limit - counts[i], max(1, left * portions[i] // whole), spare)
            counts[i] = counts[i] + addition
            spare = spare - addition
    return np.array(counts)


def normal_values(rng, dims, deviation, most, shards=(), dtype=jnp.bfloat16):
    entries = jax.random.normal(rng, dims, jnp.float32) * deviation
    if len(shards) > 0:
        entries = block_levels(rng, dims, shards, -0.22, 0.18) * entries
    return jnp.clip(entries, min=-most, max=most).astype(dtype)


def setup_inputs(seed: int = 0) -> dict:
    streams_of = jax.random.split(jax.random.key(seed), 7)
    tokens = normal_values(streams_of[0], (TOKENS, D), 1.0, 6.0, ((0, 32),))
    expert_ids_keys = jax.random.split(jax.random.fold_in(streams_of[1], 1), TOKENS // TOK_DEV)
    expert_ids_turns = jax.random.permutation(jax.random.fold_in(streams_of[1], 3), TOKENS // TOK_DEV)
    expert_ids = jax.vmap(lambda own, number: deal_out(jax.random.fold_in(streams_of[1], 2), own, number, TOK_DEV, EXPERTS, 2, MOST, 1))(expert_ids_keys, expert_ids_turns).reshape((TOKENS, 2))
    router_logits = normal_values(streams_of[2], (TOKENS, EXPERTS), 1.0, 6.0, ((0, 32),), jnp.float32)
    gate_weight = normal_values(streams_of[3], (N_ED, D, FF // GROUP), D ** -0.5, 0.078125, ((0, 32), (2, 8)))
    up_weight = normal_values(streams_of[4], (N_ED, D, FF // GROUP), D ** -0.5, 0.078125, ((0, 32), (2, 8)))
    down_weight = normal_values(streams_of[5], (N_ED, FF // GROUP, D), FF ** -0.5, 0.046875, ((0, 32), (1, 8)))
    return dict(tokens=tokens, expert_ids=expert_ids, router_logits=router_logits, gate_weight=gate_weight, up_weight=up_weight, down_weight=down_weight)


def hadamard(values):
    row_count, order_size = values.shape
    stride = 1
    while stride < order_size:
        grouped = values.reshape(row_count, order_size // (2 * stride), 2, stride)
        lower_half = grouped[:, :, 0, :]
        upper_half = grouped[:, :, 1, :]
        values = jnp.stack([lower_half + upper_half, lower_half - upper_half], axis=2).reshape(row_count, order_size)
        stride = stride * 2
    return values


def reference(tokens, expert_ids, router_logits, gate_weight, up_weight, down_weight):
    picked_logits = jnp.take_along_axis(router_logits, expert_ids, axis=1)
    first_share = 1.0 / (1.0 + jnp.exp(picked_logits[:, 1] - picked_logits[:, 0]))
    shares = jnp.stack([first_share, 1.0 - first_share], axis=1)
    mixed = jnp.zeros((TOKENS, D), jnp.float32)
    total_slots = N_ED * MOST
    for expert in range(EXPERTS):
        matches = expert_ids == expert
        chosen = jnp.any(matches, axis=1)
        weight_e = jnp.sum(jnp.where(matches, shares, 0.0), axis=1)
        ordering = jnp.argsort(jnp.where(chosen, 0, 1).astype(jnp.int32), stable=True)[:total_slots]
        routed = tokens[ordering]
        gate_full = gate_weight[expert * GROUP:(expert + 1) * GROUP].transpose(1, 0, 2).reshape(D, FF)
        up_full = up_weight[expert * GROUP:(expert + 1) * GROUP].transpose(1, 0, 2).reshape(D, FF)
        down_full = down_weight[expert * GROUP:(expert + 1) * GROUP].reshape(FF, D)
        gate_act = jnp.dot(routed, gate_full, preferred_element_type=jnp.float32)
        up_act = jnp.dot(routed, up_full, preferred_element_type=jnp.float32)
        hidden = jax.nn.silu(gate_act) * up_act
        rotated = (hadamard(hidden) * (FF ** -0.5)).astype(jnp.bfloat16)
        expert_out = jnp.dot(rotated, down_full, preferred_element_type=jnp.float32)
        scaled = expert_out * weight_e[ordering][:, None]
        mixed = mixed.at[ordering].add(scaled)
    return mixed.astype(jnp.bfloat16)
```

```python
import jax
import jax.numpy as jnp
from jax import lax
from jax.experimental import pallas as pl
from jax.experimental.pallas import tpu as pltpu
from jax.sharding import PartitionSpec as P

MESH = pl.DeviceIdType.MESH
BF16, F32 = jnp.bfloat16, jnp.float32
D = 6144
FF = 16384
EXPERTS = 4
TOK = 32
CAP = 24
NX, NY, NZ = 4, 4, 8
BLK = EXPERTS * CAP
PW = 384
PARTS = D // PW
UNITS = 256
SLICE = 768
HALF = PARTS // 2


def mod(value, count):
    return lax.rem(value + count, count)


def kernel(
    packed, gate_hbm, up_hbm, down_hbm, out,
    gate, up, down, had, ybuf, rows, core_s, core_r, a2a_s, a2a_r, back_s, rot,
    own, sib_s, sib_r, xs, xr, zs, zr, fxs, fxr, ys, yr,
    w_sem, y_ss, y_rs, z_ss, z_rs, x_ss, x_rs, s_ss, s_rs, c_ss, c_rs, a_ss, a_rs, b_ss, b_rs,
    sib_ss, sib_rs, x3_ss, x3_rs, z3_ss, z3_rs, fx_ss, fx_rs, y3_ss, y3_rs,
):
    ed, tp = lax.axis_index("ed"), lax.axis_index("tp")
    y, z = lax.div(ed, NZ), lax.rem(ed, NZ)
    x, c = lax.div(tp, 2), lax.rem(tp, 2)

    def at(x=x, y=y, z=z, c=c):
        return (y * NZ + z, x * 2 + c)

    sibling = at(c=1 - c)
    x_peer = [mod(x + i, NX) for i in range(NX)]
    y_peer = [mod(y + i, NY) for i in range(NY)]
    step_to = (at(z=mod(z + 1, NZ)), at(z=mod(z - 1, NZ)))

    def remote(src, dst, send, recv, device):
        return pltpu.make_async_remote_copy(
            src_ref=src, dst_ref=dst, send_sem=send, recv_sem=recv, device_id=device, device_id_type=MESH
        )

    sent = []

    def push(src, dst, send, recv, device):
        copy = remote(src, dst, send, recv, device)
        copy.start()
        sent.append(copy)

    def arrive(dst, send, recv):
        remote(dst, dst, send, recv, sibling).wait_recv()

    weights = [
        pltpu.make_async_copy(gate_hbm.at[0], gate, w_sem.at[0]),
        pltpu.make_async_copy(up_hbm.at[0], up, w_sem.at[1]),
        pltpu.make_async_copy(down_hbm.at[0], down, w_sem.at[2]),
    ]
    for copy in weights:
        copy.start()

    barrier = pltpu.get_barrier_semaphore()
    greeted = [sibling, *step_to]
    greeted += [at(x=x_peer[i]) for i in range(1, NX)]
    greeted += [at(y=y_peer[i]) for i in range(1, NY)]
    for device in greeted:
        pl.semaphore_signal(barrier, inc=1, device_id=device, device_id_type=MESH)
    pl.semaphore_wait(barrier, len(greeted))

    base = c * HALF
    wide, narrow = 4 * PW, PW
    shared = base + 4 + x
    cols_wide = pl.ds(pl.multiple_of(base * PW, 128), wide)
    cols_narrow = pl.ds(pl.multiple_of(shared * PW, 128), narrow)
    for i in (2, 1, 3):
        slot = pl.ds(pl.multiple_of(y_peer[i] * TOK, TOK), TOK)
        device = at(y=y_peer[i])
        push(packed.at[slot, cols_narrow], ybuf.at[y, :, pl.ds(wide, narrow)], y_ss.at[i, 0], y_rs.at[i, 0], device)
        push(packed.at[slot, cols_wide], ybuf.at[y, :, pl.ds(0, wide)], y_ss.at[i, 1], y_rs.at[i, 1], device)
    slot = pl.ds(pl.multiple_of(y * TOK, TOK), TOK)
    ybuf[y, :, 0:wide] = packed[slot, cols_wide]
    ybuf[y, :, wide:] = packed[slot, cols_narrow]

    both = lax.broadcasted_iota(jnp.int32, (UNITS, UNITS), 0) & lax.broadcasted_iota(jnp.int32, (UNITS, UNITS), 1)
    for shift in (4, 2, 1):
        both = both ^ (both >> shift)
    had[...] = (1 - 2 * (both & 1)).astype(F32).astype(BF16)

    i_row = lax.broadcasted_iota(jnp.int32, (BLK, NY * TOK), 0)
    i_col = lax.broadcasted_iota(jnp.int32, (BLK, NY * TOK), 1)
    squeeze = jnp.zeros((BLK, NY * TOK), F32)
    for s in range(NY):
        inside = (i_row >= CAP * s) & (i_row < CAP * (s + 1)) & (i_col - TOK * s == i_row - CAP * s)
        squeeze = jnp.where(inside, 1.0, squeeze)
    squeeze = squeeze.astype(BF16)

    for i in range(1, NY):
        source = y_peer[NY - i]
        arrive(ybuf.at[source, :, pl.ds(wide, narrow)], y_ss.at[i, 0], y_rs.at[i, 0])
        arrive(ybuf.at[source, :, pl.ds(0, wide)], y_ss.at[i, 1], y_rs.at[i, 1])

    def squeezed(at_col):
        block = ybuf[:, :, at_col:at_col + PW].reshape(NY * TOK, PW)
        return jnp.dot(squeeze, block, preferred_element_type=F32).astype(BF16)

    rows[z, shared] = squeezed(wide)
    for p in range(4):
        rows[z, base + p] = squeezed(p * PW)

    blocks = [z]
    for t in (1, 2, 3):
        blocks += [mod(z - t, NZ), mod(z + t, NZ)]
    blocks.append(mod(z + 4, NZ))

    def z_send(b, way, t):
        if t < 4:
            push(rows.at[b, shared], rows.at[b, shared], z_ss.at[way, t, 0], z_rs.at[way, t, 0], step_to[way])
            part = rows.at[b, pl.ds(base, 4)]
        elif way == 0:
            push(rows.at[b, shared], rows.at[b, shared], z_ss.at[way, t, 0], z_rs.at[way, t, 0], step_to[way])
            part = rows.at[b, pl.ds(base, 2)]
        else:
            part = rows.at[b, pl.ds(base + 2, 2)]
        push(part, part, z_ss.at[way, t, 1], z_rs.at[way, t, 1], step_to[way])

    def share(b, i):
        for j in (2, 1, 3):
            push(rows.at[b, shared], rows.at[b, shared], x_ss.at[i, j], x_rs.at[i, j], at(x=x_peer[j]))
        push(rows.at[b, shared], rows.at[b, shared], s_ss.at[i, 0], s_rs.at[i, 0], sibling)
        part = rows.at[b, pl.ds(base, 4)]
        push(part, part, s_ss.at[i, 4], s_rs.at[i, 4], sibling)

    def x_pass(b, i):
        for j in (1, 3, 2):
            part = rows.at[b, base + 4 + x_peer[NX - j]]
            arrive(part, x_ss.at[i, j], x_rs.at[i, j])
            push(part, part, s_ss.at[i, j], s_rs.at[i, j], sibling)

    other = (1 - c) * HALF

    def ready(b, i):
        part = rows.at[b, pl.ds(other, 4)]
        arrive(part, s_ss.at[i, 4], s_rs.at[i, 4])
        for j in range(NX):
            part = rows.at[b, other + 4 + x_peer[(NX - j) % NX]]
            arrive(part, s_ss.at[i, j], s_rs.at[i, j])

    def hidden(b):
        gate_act = jnp.zeros((BLK, UNITS), F32)
        up_act = jnp.zeros((BLK, UNITS), F32)
        for p in range(0, PARTS, 2):
            block = jnp.concatenate([rows[b, p], rows[b, p + 1]], axis=1)
            gate_act += jnp.dot(block, gate[p * PW:(p + 2) * PW, :], preferred_element_type=F32)
            up_act += jnp.dot(block, up[p * PW:(p + 2) * PW, :], preferred_element_type=F32)
        value = gate_act / (1.0 + jnp.exp(-gate_act)) * up_act
        high = value.astype(BF16)
        low = (value - high.astype(F32)).astype(BF16)
        core_s[b] = jnp.dot(high, had[...], preferred_element_type=F32) + jnp.dot(
            low, had[...], preferred_element_type=F32
        )

    def core_push(b, i):
        push(core_s.at[b], core_r.at[b], c_ss.at[i], c_rs.at[i], sibling)

    sign = (1 - 2 * c).astype(F32)
    me32 = z * NX + x

    def spread(b, i):
        arrive(core_r.at[b], c_ss.at[i], c_rs.at[i])
        value = (core_r[b] + sign * core_s[b]).astype(BF16)
        for k in range(NX):
            a2a_s[b, k] = value[48 * (k // 2):48 * (k // 2) + 48, 128 * (k % 2):128 * (k % 2) + 128]
        for j in range(NX):
            k = x_peer[j]
            if i == 0 and j == 0:
                a2a_r[me32] = a2a_s[b, k]
            else:
                push(a2a_s.at[b, k], a2a_r.at[me32], a_ss.at[i, j], a_rs.at[0], at(x=k, z=b))

    for way in (0, 1):
        z_send(z, way, 1)
    share(z, 0)

    for copy in weights[:2]:
        copy.wait()

    def group(t):
        if t == 0:
            return [0]
        return [2 * t - 1, 2 * t] if t < 4 else [7]

    for t in (1, 2, 3, 4):
        for way in (0, 1):
            i = group(t)[way] if t < 4 else 7
            b = blocks[i]
            if t < 4 or way == 0:
                arrive(rows.at[b, shared], z_ss.at[way, t, 0], z_rs.at[way, t, 0])
            if t < 4:
                part = rows.at[b, pl.ds(base, 4)]
            else:
                part = rows.at[b, pl.ds(base + 2 * way, 2)]
            arrive(part, z_ss.at[way, t, 1], z_rs.at[way, t, 1])
            if t < 4:
                z_send(b, way, t + 1)
        for i in group(t):
            share(blocks[i], i)
        for i in group(t - 1):
            x_pass(blocks[i], i)
        if t >= 2:
            for i in group(t - 2):
                spread(blocks[i], i)
        for i in group(t - 1):
            ready(blocks[i], i)
            hidden(blocks[i])
            core_push(blocks[i], i)
    x_pass(blocks[7], 7)
    for i in group(3):
        spread(blocks[i], i)
    ready(blocks[7], 7)
    hidden(blocks[7])
    core_push(blocks[7], 7)
    spread(blocks[7], 7)

    remote(a2a_r.at[pl.ds(0, 31)], a2a_r.at[pl.ds(0, 31)], a_ss.at[0, 0], a_rs.at[0], sibling).wait_recv()
    count = NZ * NX

    @pl.loop(0, 3)
    def _(r):
        piece = pl.ds(pl.multiple_of(r * 16, 16), 16)
        values = [a2a_r[s, piece, :].astype(F32) for s in range(count)]
        stride = 1
        while stride < count:
            for low in range(count):
                if low & stride == 0:
                    first, second = values[low], values[low + stride]
                    values[low], values[low + stride] = first + second, first - second
            stride *= 2
        for s in range(count):
            back_s[s, piece, :] = (values[s] * FF ** -0.5).astype(BF16)

    rot[z, x] = back_s[me32]
    for dz in (4, 3, 5, 2, 6, 1, 7, 0):
        zz = mod(z + dz, NZ)
        for j in range(NX):
            if dz + j:
                s = zz * NX + x_peer[j]
                push(back_s.at[s], rot.at[z, x], b_ss.at[dz, j], b_rs.at[z], at(x=x_peer[j], z=zz))

    weights[2].wait()
    order = [4, 3, 5, 2, 6, 1, 7, 0]
    x3_parts = [mod(x + i, NX) for i in range(NX)]

    def down_block(dz, turn):
        b = mod(z + dz, NZ)
        if dz:
            arrive(rot.at[b], b_ss.at[0, 1], b_rs.at[b])
        else:
            arrive(rot.at[b, pl.ds(0, 3)], b_ss.at[0, 1], b_rs.at[b])
        upper = jnp.concatenate([rot[b, 0], rot[b, 1]], axis=1)
        lower = jnp.concatenate([rot[b, 2], rot[b, 3]], axis=1)
        block = jnp.concatenate([upper, lower], axis=0)
        slot = turn % 2
        if turn >= 2:
            remote(sib_s.at[slot], sib_r.at[b], sib_ss.at[slot], sib_rs.at[0], sibling).wait_send()
        for k in range(NX):
            columns = pl.ds(pl.multiple_of((2 * k + 1 - c) * SLICE, 128), SLICE)
            sib_s[slot, k] = jnp.dot(block, down[:, columns], preferred_element_type=F32)
        remote(sib_s.at[slot], sib_r.at[b], sib_ss.at[slot], sib_rs.at[dz], sibling).start()
        for k in range(NX):
            columns = pl.ds(pl.multiple_of((2 * k + c) * SLICE, 128), SLICE)
            own[b, k] = jnp.dot(block, down[:, columns], preferred_element_type=F32)

    def x_scatter(dz):
        b = mod(z + dz, NZ)
        arrive(sib_r.at[b], sib_ss.at[0], sib_rs.at[dz])
        for j in (2, 1, 3):
            k = x3_parts[j]
            xs[b, j] = (own[b, k, :, 0:PW] + sib_r[b, k, :, 0:PW]).astype(BF16)
            push(xs.at[b, j], xr.at[b, j], x3_ss.at[dz, j], x3_rs.at[dz, j], at(x=k))

    def term(b, part):
        if part:
            k = part - 1
            return own[b, k, :, PW:] + sib_r[b, k, :, PW:]
        total = own[b, x, :, 0:PW] + sib_r[b, x, :, 0:PW]
        for j in range(1, NX):
            total += xr[b, j].astype(F32)
        return total

    def x_gathered(dz):
        b = mod(z + dz, NZ)
        for j in range(1, NX):
            arrive(xr.at[b, j], x3_ss.at[dz, j], x3_rs.at[dz, j])

    def far_parts(way):
        return (0, 3) if way == 0 else (3, 2)

    def chain_in(way, step):
        if step == 0:
            start, size = far_parts(way)
            arrive(zr.at[way, step, pl.ds(start, size)], z3_ss.at[way, step], z3_rs.at[way, step])
        else:
            arrive(zr.at[way, step], z3_ss.at[way, step], z3_rs.at[way, step])

    def chain(way, step):
        dz = 4 - step if way == 0 else 4 + step
        b = mod(z + dz, NZ)
        start, size = far_parts(way)
        if step:
            chain_in(way, step - 1)
        for part in range(5):
            received = start <= part < start + size
            if step == 0 and not received:
                continue
            total = term(b, part)
            if step > 1 or (step == 1 and received):
                total += zr[way, step - 1, part].astype(F32)
            zs[way, step, part] = total.astype(BF16)
        if step == 0:
            src, dst = zs.at[way, step, pl.ds(start, size)], zr.at[way, step, pl.ds(start, size)]
        else:
            src, dst = zs.at[way, step], zr.at[way, step]
        push(src, dst, z3_ss.at[way, step], z3_rs.at[way, step], step_to[way])

    down_block(4, 0)
    down_block(3, 1)
    x_scatter(4)
    down_block(5, 2)
    x_scatter(3)
    x_gathered(4)
    chain(0, 0)
    chain(1, 0)
    down_block(2, 3)
    x_scatter(5)
    down_block(6, 4)
    x_scatter(2)
    x_gathered(3)
    chain(0, 1)
    x_gathered(5)
    chain(1, 1)
    down_block(1, 5)
    x_scatter(6)
    down_block(7, 6)
    x_scatter(1)
    down_block(0, 7)
    x_scatter(7)
    x_gathered(2)
    chain(0, 2)
    x_gathered(6)
    chain(1, 2)
    x_scatter(0)
    x_gathered(1)
    chain(0, 3)
    x_gathered(7)
    chain(1, 3)
    x_gathered(0)
    chain_in(0, 3)
    chain_in(1, 3)

    def final(part):
        return term(z, part) + (zr[0, 3, part].astype(F32) + zr[1, 3, part].astype(F32))

    for k in range(NX):
        fxs[k] = final(1 + k).astype(BF16)
    for j in (2, 1, 3):
        k = x_peer[j]
        push(fxs.at[k], fxr.at[j], fx_ss.at[j], fx_rs.at[j], at(x=k))

    def y_send(half):
        for i in (2, 1, 3):
            span = pl.ds(pl.multiple_of(y_peer[i] * CAP, 8), CAP)
            push(ys.at[half, span], yr.at[half, y], y3_ss.at[half, i], y3_rs.at[half, i], at(y=y_peer[i]))
        yr[half, y] = ys[half, pl.ds(pl.multiple_of(y * CAP, 8), CAP)]

    ys[0] = final(0)
    y_send(0)
    total = own[z, x, :, PW:] + sib_r[z, x, :, PW:]
    total += zr[0, 3, 1 + x].astype(F32) + zr[1, 3, 1 + x].astype(F32)
    for j in range(1, NX):
        arrive(fxr.at[j], fx_ss.at[j], fx_rs.at[j])
        total += fxr[j].astype(F32)
    ys[1] = total
    y_send(1)
    for half in (0, 1):
        for i in range(1, NY):
            source = y_peer[NY - i]
            arrive(yr.at[half, source], y3_ss.at[half, i], y3_rs.at[half, i])
        for e in range(EXPERTS):
            out[e * CAP:(e + 1) * CAP, half * PW:(half + 1) * PW] = yr[half, e]
    for copy in sent:
        copy.wait_send()
    for slot in (0, 1):
        remote(sib_s.at[slot], sib_r.at[0], sib_ss.at[slot], sib_rs.at[0], sibling).wait_send()


def run(packed, gate_weight, up_weight, down_weight):
    vmem, dma = pltpu.VMEM, pltpu.SemaphoreType.DMA
    scratch = [
        vmem((D, UNITS), BF16), vmem((D, UNITS), BF16), vmem((UNITS, D), BF16),
        vmem((UNITS, UNITS), BF16),
        vmem((NY, TOK, 5 * PW), BF16),
        vmem((NZ, PARTS, BLK, PW), BF16),
        vmem((NZ, BLK, UNITS), F32), vmem((NZ, BLK, UNITS), F32),
        vmem((NZ, NX, 48, 128), BF16),
        vmem((NZ * NX, 48, 128), BF16), vmem((NZ * NX, 48, 128), BF16),
        vmem((NZ, NX, 48, 128), BF16),
        vmem((NZ, NX, BLK, SLICE), F32),
        vmem((2, NX, BLK, SLICE), F32),
        vmem((NZ, NX, BLK, SLICE), F32),
        vmem((NZ, NX, BLK, PW), BF16), vmem((NZ, NX, BLK, PW), BF16),
        vmem((2, 4, 5, BLK, PW), BF16), vmem((2, 4, 5, BLK, PW), BF16),
        vmem((NX, BLK, PW), BF16), vmem((NX, BLK, PW), BF16),
        vmem((2, BLK, PW), F32), vmem((2, NY, CAP, PW), F32),
        dma((3,)),
        dma((NY, 2)), dma((NY, 2)),
        dma((2, 5, 2)), dma((2, 5, 2)),
        dma((NZ, NX)), dma((NZ, NX)),
        dma((NZ, 5)), dma((NZ, 5)),
        dma((NZ,)), dma((NZ,)),
        dma((NZ, NX)), dma((1,)),
        dma((NZ, NX)), dma((NZ,)),
        dma((2,)), dma((NZ,)),
        dma((NZ, NX)), dma((NZ, NX)),
        dma((2, 4)), dma((2, 4)),
        dma((NX,)), dma((NX,)),
        dma((2, NY)), dma((2, NY)),
    ]
    return pl.pallas_call(
        kernel,
        out_shape=jax.ShapeDtypeStruct((BLK, SLICE), F32),
        in_specs=[pl.BlockSpec(memory_space=pltpu.VMEM)] + [pl.BlockSpec(memory_space=pl.ANY)] * 3,
        out_specs=pl.BlockSpec(memory_space=pltpu.VMEM),
        scratch_shapes=scratch,
        compiler_params=pltpu.CompilerParams(
            collective_id=1, has_side_effects=True, vmem_limit_bytes=63 * 2 ** 20
        ),
        name="experts",
    )(packed, gate_weight, up_weight, down_weight)


def on_device(tokens, expert_ids, router_logits, gate_weight, up_weight, down_weight):
    expert_range = jnp.arange(EXPERTS, dtype=jnp.int32)
    picked = expert_ids[:, :, None] == expert_range[None, None, :]
    chosen = jnp.any(picked, axis=1).astype(jnp.int32)
    slot_index = jnp.cumsum(chosen, axis=0) - chosen
    slot_range = jnp.arange(TOK, dtype=jnp.int32)
    placing = (chosen[:, :, None] == 1) & (slot_index[:, :, None] == slot_range[None, None, :])
    packed = jnp.einsum(
        "tem,td->emd", placing.astype(BF16), tokens, preferred_element_type=F32
    ).astype(BF16)
    returned = run(packed.reshape(EXPERTS * TOK, D), gate_weight, up_weight, down_weight)
    picked_logits = jnp.sum(jnp.where(picked, router_logits[:, None, :], 0.0), axis=2)
    first_share = 1.0 / (1.0 + jnp.exp(picked_logits[:, 1] - picked_logits[:, 0]))
    shares = jnp.stack([first_share, 1.0 - first_share], axis=1)
    weight_e = jnp.sum(jnp.where(picked, shares[:, :, None], 0.0), axis=1)
    combine = jnp.where(placing[:, :, :CAP], weight_e[:, :, None], 0.0).reshape(TOK, EXPERTS * CAP)
    output = lax.dot_general(
        combine, returned, (((1,), (0,)), ((), ())), precision=lax.Precision.HIGHEST
    )
    return output.astype(BF16)


def solution(mesh):
    placed = (
        P("ed", None),
        P("ed", None),
        P("ed", None),
        P("ed", None, "tp"),
        P("ed", None, "tp"),
        P("ed", "tp", None),
    )
    return jax.shard_map(
        on_device, mesh=mesh, in_specs=placed, out_specs=P("ed", "tp"), check_vma=False
    )
```

```python
import jax
import jax.numpy as jnp
from jax import lax
from jax.experimental import pallas as pl
from jax.experimental.pallas import tpu as pltpu
from jax.sharding import PartitionSpec as P

MESH = pl.DeviceIdType.MESH
BF16, F32 = jnp.bfloat16, jnp.float32
D = 6144
FF = 16384
EXPERTS = 4
TOK = 32
CAP = 24
NX, NY, NZ = 4, 4, 8
BLK = EXPERTS * CAP
PW = 384
PARTS = D // PW
UNITS = 256
SLICE = 768
HALF = PARTS // 2


def mod(value, count):
    return lax.rem(value + count, count)


def kernel(
    tokens_hbm, expert_ids, router_logits, gate_hbm, up_hbm, down_hbm, out,
    tokens, packed, gate, up, down, had, ybuf, rows, core_s, core_r, a2a_s, a2a_r, wide_r, back_s, rot,
    own, sib_s, sib_r, xs, xr, zs, zr, fxs, fxr, ys, yr,
    t_sem, w_sem, y_ss, y_rs, z_ss, z_rs, x_ss, x_rs, s_ss, s_rs, c_ss, c_rs, a_ss, a_rs, b_ss, b_rs,
    sib_ss, sib_rs, x3_ss, x3_rs, z3_ss, z3_rs, fx_ss, fx_rs, y3_ss, y3_rs,
):
    ed, tp = lax.axis_index("ed"), lax.axis_index("tp")
    y, z = lax.div(ed, NZ), lax.rem(ed, NZ)
    x, c = lax.div(tp, 2), lax.rem(tp, 2)

    def at(x=x, y=y, z=z, c=c):
        return (y * NZ + z, x * 2 + c)

    sibling = at(c=1 - c)
    x_peer = [mod(x + i, NX) for i in range(NX)]
    y_peer = [mod(y + i, NY) for i in range(NY)]
    step_to = (at(z=mod(z + 1, NZ)), at(z=mod(z - 1, NZ)))

    def remote(src, dst, send, recv, device):
        return pltpu.make_async_remote_copy(
            src_ref=src, dst_ref=dst, send_sem=send, recv_sem=recv, device_id=device, device_id_type=MESH
        )

    sent = []

    def push(src, dst, send, recv, device):
        copy = remote(src, dst, send, recv, device)
        copy.start()
        sent.append(copy)

    def arrive(dst, send, recv):
        remote(dst, dst, send, recv, sibling).wait_recv()

    tokens_copy = pltpu.make_async_copy(tokens_hbm, tokens, t_sem)
    tokens_copy.start()
    weights = [
        pltpu.make_async_copy(gate_hbm.at[0], gate, w_sem.at[0]),
        pltpu.make_async_copy(up_hbm.at[0], up, w_sem.at[1]),
        pltpu.make_async_copy(down_hbm.at[0], down, w_sem.at[2]),
    ]
    for copy in weights:
        copy.start()

    barrier = pltpu.get_barrier_semaphore()
    greeted = [sibling, *step_to]
    greeted += [at(x=x_peer[i]) for i in range(1, NX)]
    greeted += [at(y=y_peer[i]) for i in range(1, NY)]
    for device in greeted:
        pl.semaphore_signal(barrier, inc=1, device_id=device, device_id_type=MESH)
    pl.semaphore_wait(barrier, len(greeted))

    tok_row = lax.broadcasted_iota(jnp.int32, (TOK, TOK), 0)
    tok_col = lax.broadcasted_iota(jnp.int32, (TOK, TOK), 1)
    before = (tok_row > tok_col).astype(F32).astype(BF16)

    def column(values):
        return jnp.sum(jnp.where(tok_row == tok_col, values, jnp.zeros_like(values)), axis=1, keepdims=True)

    first, second = column(expert_ids[0:1, :]), column(expert_ids[1:2, :])

    def place(capacity):
        lane = lax.broadcasted_iota(jnp.int32, (TOK, EXPERTS * capacity), 1)
        expert = jnp.zeros_like(lane)
        for e in range(1, EXPERTS):
            expert += (lane >= e * capacity).astype(jnp.int32)
        chosen = (first == expert) | (second == expert)
        count = jnp.dot(before, chosen.astype(F32).astype(BF16), preferred_element_type=F32)
        return expert, chosen & (count == (lane - expert * capacity).astype(F32))

    _, placing = place(TOK)
    placing = placing.astype(F32).astype(BF16)

    base = c * HALF
    wide, narrow = 4 * PW, PW
    shared = base + 4 + x
    cols_wide = pl.ds(pl.multiple_of(base * PW, 128), wide)
    cols_narrow = pl.ds(pl.multiple_of(shared * PW, 128), narrow)
    tokens_copy.wait()
    for kind, columns, span in ((0, cols_narrow, pl.ds(wide, narrow)), (1, cols_wide, pl.ds(0, wide))):
        packed[:, span] = lax.dot_general(
            placing, tokens[:, columns], (((0,), (0,)), ((), ())), preferred_element_type=F32
        ).astype(BF16)
        for i in (2, 1, 3):
            slot = pl.ds(pl.multiple_of(y_peer[i] * TOK, TOK), TOK)
            push(packed.at[slot, span], ybuf.at[y, :, span], y_ss.at[i, kind], y_rs.at[i, kind], at(y=y_peer[i]))
    ybuf[y] = packed[pl.ds(pl.multiple_of(y * TOK, TOK), TOK), :]

    both = lax.broadcasted_iota(jnp.int32, (UNITS, UNITS), 0) & lax.broadcasted_iota(jnp.int32, (UNITS, UNITS), 1)
    for shift in (4, 2, 1):
        both = both ^ (both >> shift)
    had[...] = (1 - 2 * (both & 1)).astype(F32).astype(BF16)

    i_row = lax.broadcasted_iota(jnp.int32, (BLK, NY * TOK), 0)
    i_col = lax.broadcasted_iota(jnp.int32, (BLK, NY * TOK), 1)
    squeeze = jnp.zeros((BLK, NY * TOK), F32)
    for s in range(NY):
        inside = (i_row >= CAP * s) & (i_row < CAP * (s + 1)) & (i_col - TOK * s == i_row - CAP * s)
        squeeze = jnp.where(inside, 1.0, squeeze)
    squeeze = squeeze.astype(BF16)

    blocks = [z]
    for t in (1, 2, 3):
        blocks += [mod(z - t, NZ), mod(z + t, NZ)]
    blocks.append(mod(z + 4, NZ))

    def parts_of(b, g):
        return rows.at[b, shared] if g == 0 else rows.at[b, pl.ds(base + 2 * (g - 1), 2)]

    def goes(way, t, g):
        return t < 4 or (g < 2) == (way == 0)

    def z_send(b, way, t, g):
        if t <= 4 and goes(way, t, g):
            part = parts_of(b, g)
            push(part, part, z_ss.at[way, t, g], z_rs.at[way, t, g], step_to[way])

    def share(b, i, g):
        part = parts_of(b, g)
        if g == 0:
            for j in (2, 1, 3):
                push(part, part, x_ss.at[i, j], x_rs.at[i, j], at(x=x_peer[j]))
        push(part, part, s_ss.at[i, 3 + g], s_rs.at[i, 3 + g], sibling)

    def x_pass(b, i):
        for j in (1, 3, 2):
            part = rows.at[b, base + 4 + x_peer[NX - j]]
            arrive(part, x_ss.at[i, j], x_rs.at[i, j])
            push(part, part, s_ss.at[i, j - 1], s_rs.at[i, j - 1], sibling)

    other = (1 - c) * HALF

    def ready(b, i):
        arrive(rows.at[b, other + 4 + x], s_ss.at[i, 3], s_rs.at[i, 3])
        for g in (1, 2):
            arrive(rows.at[b, pl.ds(other + 2 * (g - 1), 2)], s_ss.at[i, 3 + g], s_rs.at[i, 3 + g])
        for j in range(1, NX):
            part = rows.at[b, other + 4 + x_peer[NX - j]]
            arrive(part, s_ss.at[i, j - 1], s_rs.at[i, j - 1])

    def hidden(b):
        gate_act = jnp.zeros((BLK, UNITS), F32)
        up_act = jnp.zeros((BLK, UNITS), F32)
        for p in range(0, PARTS, 2):
            block = jnp.concatenate([rows[b, p], rows[b, p + 1]], axis=1)
            gate_act += jnp.dot(block, gate[p * PW:(p + 2) * PW, :], preferred_element_type=F32)
            up_act += jnp.dot(block, up[p * PW:(p + 2) * PW, :], preferred_element_type=F32)
        value = gate_act / (1.0 + jnp.exp(-gate_act)) * up_act
        high = value.astype(BF16)
        low = (value - high.astype(F32)).astype(BF16)
        core_s[b] = jnp.dot(high, had[...], preferred_element_type=F32) + jnp.dot(
            low, had[...], preferred_element_type=F32
        )

    def core_push(b, i):
        push(core_s.at[b], core_r.at[b], c_ss.at[i], c_rs.at[i], sibling)

    sign = (1 - 2 * c).astype(F32)
    me32 = z * NX + x

    def spread(b, i):
        arrive(core_r.at[b], c_ss.at[i], c_rs.at[i])
        value = (core_r[b] + sign * core_s[b]).astype(BF16)
        for k in range(NX):
            a2a_s[b, k] = value[48 * (k // 2):48 * (k // 2) + 48, 128 * (k % 2):128 * (k % 2) + 128]
        for j in range(NX):
            k = x_peer[j]
            if i == 0 and j == 0:
                a2a_r[me32] = a2a_s[b, k]
            else:
                push(a2a_s.at[b, k], a2a_r.at[me32], a_ss.at[i, j], a_rs.at[0], at(x=k, z=b))

    def squeezed(at_col):
        block = ybuf[:, :, at_col:at_col + PW].reshape(NY * TOK, PW)
        return jnp.dot(squeeze, block, preferred_element_type=F32).astype(BF16)

    ahead = []
    for g in (0, 1, 2):
        if g < 2:
            span = pl.ds(wide, narrow) if g == 0 else pl.ds(0, wide)
            for i in range(1, NY):
                arrive(ybuf.at[y_peer[NY - i], :, span], y_ss.at[i, g], y_rs.at[i, g])
        if g == 0:
            rows[z, shared] = squeezed(wide)
        else:
            for p in (2 * g - 2, 2 * g - 1):
                rows[z, base + p] = squeezed(p * PW)
        if g == 2:
            for copy in ahead:
                copy.wait_send()
        for way in (0, 1):
            z_send(z, way, 1, g)
            ahead.append(sent.pop())
        share(z, 0, g)

    sent.extend(ahead[4:])
    for copy in weights[:2]:
        copy.wait()

    def group(t):
        if t == 0:
            return [0]
        return [2 * t - 1, 2 * t] if t < 4 else [7]

    def work(i):
        ready(blocks[i], i)
        hidden(blocks[i])
        core_push(blocks[i], i)

    for t in (1, 2, 3, 4):
        for g in (0, 1, 2):
            for way in (0, 1):
                if not goes(way, t, g):
                    continue
                i = group(t)[way] if t < 4 else 7
                b = blocks[i]
                arrive(parts_of(b, g), z_ss.at[way, t, g], z_rs.at[way, t, g])
                z_send(b, way, t + 1, g)
                share(b, i, g)
            if g == 0 and t >= 2:
                for i in group(t - 2):
                    spread(blocks[i], i)
            if g == 1:
                for i in group(t - 1):
                    x_pass(blocks[i], i)
            if 0 < g <= len(group(t - 1)):
                work(group(t - 1)[g - 1])
    x_pass(blocks[7], 7)
    for i in group(3):
        spread(blocks[i], i)
    work(7)
    spread(blocks[7], 7)

    remote(a2a_r.at[pl.ds(0, 31)], a2a_r.at[pl.ds(0, 31)], a_ss.at[0, 0], a_rs.at[0], sibling).wait_recv()
    count = NZ * NX

    def butterfly(values):
        stride = 1
        while stride < len(values):
            for low in range(len(values)):
                if low & stride == 0:
                    upper, lower = values[low], values[low + stride]
                    values[low], values[low + stride] = upper + lower, upper - lower
            stride *= 2
        return values

    for r in range(0, 48, 16):
        for s in range(0, count, 8):
            values = butterfly([a2a_r[s + n, r:r + 16, :].astype(F32) for n in range(8)])
            for n in range(8):
                wide_r[s + n, r:r + 16, :] = values[n]
        for n in range(8):
            values = butterfly([wide_r[n + 8 * q, r:r + 16, :] for q in range(4)])
            for q in range(4):
                back_s[n + 8 * q, r:r + 16, :] = (values[q] * FF ** -0.5).astype(BF16)

    rot[z, x] = back_s[me32]
    for dz in (4, 3, 5, 2, 6, 1, 7, 0):
        zz = mod(z + dz, NZ)
        for j in range(NX):
            if dz + j:
                s = zz * NX + x_peer[j]
                push(back_s.at[s], rot.at[z, x], b_ss.at[dz, j], b_rs.at[z], at(x=x_peer[j], z=zz))

    weights[2].wait()
    order = [4, 3, 5, 2, 6, 1, 7, 0]
    x3_parts = [mod(x + i, NX) for i in range(NX)]

    def down_block(dz, turn):
        b = mod(z + dz, NZ)
        if dz:
            arrive(rot.at[b], b_ss.at[0, 1], b_rs.at[b])
        else:
            arrive(rot.at[b, pl.ds(0, 3)], b_ss.at[0, 1], b_rs.at[b])
        upper = jnp.concatenate([rot[b, 0], rot[b, 1]], axis=1)
        lower = jnp.concatenate([rot[b, 2], rot[b, 3]], axis=1)
        block = jnp.concatenate([upper, lower], axis=0)
        slot = turn % 2
        if turn >= 2:
            remote(sib_s.at[slot], sib_r.at[b], sib_ss.at[slot], sib_rs.at[0], sibling).wait_send()
        for k in range(NX):
            columns = pl.ds(pl.multiple_of((2 * k + 1 - c) * SLICE, 128), SLICE)
            sib_s[slot, k] = jnp.dot(block, down[:, columns], preferred_element_type=F32)
        remote(sib_s.at[slot], sib_r.at[b], sib_ss.at[slot], sib_rs.at[dz], sibling).start()
        for k in range(NX):
            columns = pl.ds(pl.multiple_of((2 * k + c) * SLICE, 128), SLICE)
            own[b, k] = jnp.dot(block, down[:, columns], preferred_element_type=F32)

    def x_scatter(dz):
        b = mod(z + dz, NZ)
        arrive(sib_r.at[b], sib_ss.at[0], sib_rs.at[dz])
        for j in (2, 1, 3):
            k = x3_parts[j]
            xs[b, j] = (own[b, k, :, 0:PW] + sib_r[b, k, :, 0:PW]).astype(BF16)
            push(xs.at[b, j], xr.at[b, j], x3_ss.at[dz, j], x3_rs.at[dz, j], at(x=k))

    def term(b, part):
        if part:
            k = part - 1
            return own[b, k, :, PW:] + sib_r[b, k, :, PW:]
        total = own[b, x, :, 0:PW] + sib_r[b, x, :, 0:PW]
        for j in range(1, NX):
            total += xr[b, j].astype(F32)
        return total

    def x_gathered(dz):
        b = mod(z + dz, NZ)
        for j in range(1, NX):
            arrive(xr.at[b, j], x3_ss.at[dz, j], x3_rs.at[dz, j])

    def far(way, part):
        return (part < 3) == (way == 0)

    def chain_in(way, step, part):
        arrive(zr.at[way, step, part], z3_ss.at[way, step, part], z3_rs.at[way, step, part])

    def chain(step, parts):
        for part in parts:
            for way in (0, 1):
                if step == 0 and not far(way, part):
                    continue
                total = term(mod(z + (4 - step if way == 0 else 4 + step), NZ), part)
                if step > 1 or (step == 1 and far(way, part)):
                    chain_in(way, step - 1, part)
                    total += zr[way, step - 1, part].astype(F32)
                zs[way, step, part] = total.astype(BF16)
                push(
                    zs.at[way, step, part], zr.at[way, step, part],
                    z3_ss.at[way, step, part], z3_rs.at[way, step, part], step_to[way],
                )

    down_block(4, 0)
    down_block(3, 1)
    x_scatter(4)
    chain(0, (1, 3, 2, 4))
    down_block(5, 2)
    x_scatter(3)
    down_block(2, 3)
    x_scatter(5)
    x_gathered(4)
    chain(0, (0,))
    chain(1, (1, 2, 3, 4))
    down_block(6, 4)
    x_scatter(2)
    down_block(1, 5)
    x_gathered(3)
    x_gathered(5)
    chain(1, (0,))
    x_scatter(6)
    chain(2, (1, 2, 3, 4))
    down_block(7, 6)
    x_scatter(1)
    down_block(0, 7)
    x_gathered(2)
    x_gathered(6)
    chain(2, (0,))
    x_scatter(7)
    chain(3, (1, 2, 3, 4))
    x_scatter(0)
    x_gathered(1)
    x_gathered(7)
    chain(3, (0,))
    x_gathered(0)

    def final(part):
        return term(z, part) + (zr[0, 3, part].astype(F32) + zr[1, 3, part].astype(F32))

    for k in range(NX):
        for way in (0, 1):
            chain_in(way, 3, 1 + k)
        fxs[k] = final(1 + k).astype(BF16)
    for j in (2, 1, 3):
        k = x_peer[j]
        push(fxs.at[k], fxr.at[j], fx_ss.at[j], fx_rs.at[j], at(x=k))

    def y_send(half):
        for i in (2, 1, 3):
            span = pl.ds(pl.multiple_of(y_peer[i] * CAP, 8), CAP)
            push(ys.at[half, span], yr.at[half, y], y3_ss.at[half, i], y3_rs.at[half, i], at(y=y_peer[i]))
        yr[half, y] = ys[half, pl.ds(pl.multiple_of(y * CAP, 8), CAP)]

    for way in (0, 1):
        chain_in(way, 3, 0)
    ys[0] = final(0)
    y_send(0)
    total = own[z, x, :, PW:] + sib_r[z, x, :, PW:]
    total += zr[0, 3, 1 + x].astype(F32) + zr[1, 3, 1 + x].astype(F32)

    logits = [column(router_logits[e:e + 1, :]) for e in range(EXPERTS)]
    picked = []
    for ids in (first, second):
        value = logits[0]
        for e in range(1, EXPERTS):
            value = jnp.where(ids == e, logits[e], value)
        picked.append(value)
    share0 = 1.0 / (1.0 + jnp.exp(picked[1] - picked[0]))
    expert, placed = place(CAP)
    combine = jnp.where(placed, jnp.where(first == expert, share0, 1.0 - share0), 0.0)

    for j in range(1, NX):
        arrive(fxr.at[j], fx_ss.at[j], fx_rs.at[j])
        total += fxr[j].astype(F32)
    ys[1] = total
    y_send(1)
    for half in (0, 1):
        for i in range(1, NY):
            source = y_peer[NY - i]
            arrive(yr.at[half, source], y3_ss.at[half, i], y3_rs.at[half, i])
        out[:, half * PW:(half + 1) * PW] = jnp.dot(
            combine, yr[half].reshape(EXPERTS * CAP, PW), precision=lax.Precision.HIGHEST, preferred_element_type=F32
        ).astype(BF16)
    for copy in sent:
        copy.wait_send()
    for slot in (0, 1):
        remote(sib_s.at[slot], sib_r.at[0], sib_ss.at[slot], sib_rs.at[0], sibling).wait_send()


def run(tokens, expert_ids, router_logits, gate_weight, up_weight, down_weight):
    vmem, dma = pltpu.VMEM, pltpu.SemaphoreType.DMA
    scratch = [
        vmem((TOK, D), BF16), vmem((EXPERTS * TOK, 5 * PW), BF16),
        vmem((D, UNITS), BF16), vmem((D, UNITS), BF16), vmem((UNITS, D), BF16),
        vmem((UNITS, UNITS), BF16),
        vmem((NY, TOK, 5 * PW), BF16),
        vmem((NZ, PARTS, BLK, PW), BF16),
        vmem((NZ, BLK, UNITS), F32), vmem((NZ, BLK, UNITS), F32),
        vmem((NZ, NX, 48, 128), BF16),
        vmem((NZ * NX, 48, 128), BF16),
        vmem((NZ * NX, 48, 128), F32), vmem((NZ * NX, 48, 128), BF16),
        vmem((NZ, NX, 48, 128), BF16),
        vmem((NZ, NX, BLK, SLICE), F32),
        vmem((2, NX, BLK, SLICE), F32),
        vmem((NZ, NX, BLK, SLICE), F32),
        vmem((NZ, NX, BLK, PW), BF16), vmem((NZ, NX, BLK, PW), BF16),
        vmem((2, 4, 5, BLK, PW), BF16), vmem((2, 4, 5, BLK, PW), BF16),
        vmem((NX, BLK, PW), BF16), vmem((NX, BLK, PW), BF16),
        vmem((2, BLK, PW), F32), vmem((2, NY, CAP, PW), F32),
        dma, dma((3,)),
        dma((NY, 2)), dma((NY, 2)),
        dma((2, 5, 3)), dma((2, 5, 3)),
        dma((NZ, NX)), dma((NZ, NX)),
        dma((NZ, 6)), dma((NZ, 6)),
        dma((NZ,)), dma((NZ,)),
        dma((NZ, NX)), dma((1,)),
        dma((NZ, NX)), dma((NZ,)),
        dma((2,)), dma((NZ,)),
        dma((NZ, NX)), dma((NZ, NX)),
        dma((2, 4, 5)), dma((2, 4, 5)),
        dma((NX,)), dma((NX,)),
        dma((2, NY)), dma((2, NY)),
    ]
    return pl.pallas_call(
        kernel,
        out_shape=jax.ShapeDtypeStruct((TOK, SLICE), BF16),
        in_specs=[pl.BlockSpec(memory_space=pl.ANY)]
        + [pl.BlockSpec(memory_space=pltpu.VMEM)] * 2
        + [pl.BlockSpec(memory_space=pl.ANY)] * 3,
        out_specs=pl.BlockSpec(memory_space=pltpu.VMEM),
        scratch_shapes=scratch,
        compiler_params=pltpu.CompilerParams(
            collective_id=1, has_side_effects=True, vmem_limit_bytes=63 * 2 ** 20
        ),
        name="experts",
    )(tokens, expert_ids.T, router_logits.T, gate_weight, up_weight, down_weight)


def solution(mesh):
    placed = (
        P("ed", None),
        P("ed", None),
        P("ed", None),
        P("ed", None, "tp"),
        P("ed", None, "tp"),
        P("ed", "tp", None),
    )
    return jax.shard_map(
        run, mesh=mesh, in_specs=placed, out_specs=P("ed", "tp"), check_vma=False
    )
```

```python
import jax
import jax.numpy as jnp
from jax import lax
from jax.experimental import pallas as pl
from jax.experimental.pallas import tpu as pltpu
from jax.sharding import PartitionSpec as P

MESH = pl.DeviceIdType.MESH
BF16, F32 = jnp.bfloat16, jnp.float32
D = 6144
FF = 16384
EXPERTS = 4
TOK = 32
CAP = 24
NX, NY, NZ = 4, 4, 8
BLK = EXPERTS * CAP
PW = 512
PARTS = D // PW
UNITS = 256
SLICE = 768
HALF = PARTS // 2
HB = BLK // 2
ZW = SLICE - PW


def mod(value, count):
    return lax.rem(value + count, count)


def kernel(
    tokens_hbm, expert_ids, router_logits, gate_hbm, up_hbm, down_hbm, out,
    tokens, packed, gate, up, down, had, ybuf, rows, core_s, core_r, a2a_s, a2a_r, wide_r, back_s, rot,
    own, sib_s, sib_r, xs, xr, zs, zr, fxf, fxs, fxr, ysa, ysb, yra, yrb,
    t_sem, w_sem, y_ss, y_rs, z_ss, z_rs, x_ss, x_rs, s_ss, s_rs, c_ss, c_rs, a_ss, a_rs, b_ss, b_rs,
    sib_ss, sib_rs, x3_ss, x3_rs, z3_ss, z3_rs, fx_ss, fx_rs, y3_ss, y3_rs,
):
    ed, tp = lax.axis_index("ed"), lax.axis_index("tp")
    y, z = lax.div(ed, NZ), lax.rem(ed, NZ)
    x, c = lax.div(tp, 2), lax.rem(tp, 2)

    def at(x=x, y=y, z=z, c=c):
        return (y * NZ + z, x * 2 + c)

    sibling = at(c=1 - c)
    x_peer = [mod(x + i, NX) for i in range(NX)]
    y_peer = [mod(y + i, NY) for i in range(NY)]
    step_to = (at(z=mod(z + 1, NZ)), at(z=mod(z - 1, NZ)))

    def remote(src, dst, send, recv, device):
        return pltpu.make_async_remote_copy(
            src_ref=src, dst_ref=dst, send_sem=send, recv_sem=recv, device_id=device, device_id_type=MESH
        )

    sent = []

    def push(src, dst, send, recv, device):
        copy = remote(src, dst, send, recv, device)
        copy.start()
        sent.append(copy)

    def arrive(dst, send, recv):
        remote(dst, dst, send, recv, sibling).wait_recv()

    tokens_copy = pltpu.make_async_copy(tokens_hbm, tokens, t_sem)
    tokens_copy.start()
    weights = [
        pltpu.make_async_copy(gate_hbm.at[0], gate, w_sem.at[0]),
        pltpu.make_async_copy(up_hbm.at[0], up, w_sem.at[1]),
        pltpu.make_async_copy(down_hbm.at[0], down, w_sem.at[2]),
    ]
    for copy in weights:
        copy.start()

    barrier = pltpu.get_barrier_semaphore()
    greeted = [sibling, *step_to]
    greeted += [at(x=x_peer[i]) for i in range(1, NX)]
    greeted += [at(y=y_peer[i]) for i in range(1, NY)]
    greeted += [at(x=x_peer[i], z=mod(z + dz, NZ)) for dz in (3, 4, 5) for i in range(NX)]
    for device in greeted:
        pl.semaphore_signal(barrier, inc=1, device_id=device, device_id_type=MESH)

    tok_row = lax.broadcasted_iota(jnp.int32, (TOK, TOK), 0)
    tok_col = lax.broadcasted_iota(jnp.int32, (TOK, TOK), 1)
    before = (tok_row > tok_col).astype(F32).astype(BF16)

    def column(values):
        return jnp.sum(jnp.where(tok_row == tok_col, values, jnp.zeros_like(values)), axis=1, keepdims=True)

    first, second = column(expert_ids[0:1, :]), column(expert_ids[1:2, :])

    def place(capacity):
        lane = lax.broadcasted_iota(jnp.int32, (TOK, EXPERTS * capacity), 1)
        expert = jnp.zeros_like(lane)
        for e in range(1, EXPERTS):
            expert += (lane >= e * capacity).astype(jnp.int32)
        chosen = (first == expert) | (second == expert)
        count = jnp.dot(before, chosen.astype(F32).astype(BF16), preferred_element_type=F32)
        return expert, chosen & (count == (lane - expert * capacity).astype(F32))

    _, placing = place(TOK)
    placing = placing.astype(F32).astype(BF16)

    base = c * HALF
    wide, narrow = 2 * PW, PW
    shared = base + 2 + x
    cols_wide = pl.ds(pl.multiple_of(base * PW, 128), wide)
    cols_narrow = pl.ds(pl.multiple_of(shared * PW, 128), narrow)
    tokens_copy.wait()
    kinds = ((0, cols_narrow, pl.ds(wide, narrow)), (1, cols_wide, pl.ds(0, wide)))
    for _, columns, span in kinds:
        packed[:, span] = lax.dot_general(
            placing, tokens[:, columns], (((0,), (0,)), ((), ())), preferred_element_type=F32
        ).astype(BF16)
    pl.semaphore_wait(barrier, len(greeted))
    for kind, _, span in kinds:
        for i in (2, 1, 3):
            slot = pl.ds(pl.multiple_of(y_peer[i] * TOK, TOK), TOK)
            push(packed.at[slot, span], ybuf.at[y, :, span], y_ss.at[i, kind], y_rs.at[i, kind], at(y=y_peer[i]))
    ybuf[y] = packed[pl.ds(pl.multiple_of(y * TOK, TOK), TOK), :]

    both = lax.broadcasted_iota(jnp.int32, (UNITS, UNITS), 0) & lax.broadcasted_iota(jnp.int32, (UNITS, UNITS), 1)
    for shift in (4, 2, 1):
        both = both ^ (both >> shift)
    had[...] = (1 - 2 * (both & 1)).astype(F32).astype(BF16)

    i_row = lax.broadcasted_iota(jnp.int32, (BLK, NY * TOK), 0)
    i_col = lax.broadcasted_iota(jnp.int32, (BLK, NY * TOK), 1)
    squeeze = jnp.zeros((BLK, NY * TOK), F32)
    for s in range(NY):
        inside = (i_row >= CAP * s) & (i_row < CAP * (s + 1)) & (i_col - TOK * s == i_row - CAP * s)
        squeeze = jnp.where(inside, 1.0, squeeze)
    squeeze = squeeze.astype(BF16)

    blocks = [z]
    for t in (1, 2, 3):
        blocks += [mod(z - t, NZ), mod(z + t, NZ)]
    blocks.append(mod(z + 4, NZ))

    def part_of(b, g):
        return rows.at[b, shared if g == 0 else base + g - 1]

    def z_part(b, way, t, g):
        if t == 4 and g == 1:
            return rows.at[b, base, pl.ds(HB * way, HB)]
        return part_of(b, g)

    def goes(way, t, g):
        return t < 4 or g == 1 or (g == 0) == (way == 0)

    def z_send(b, way, t, g):
        if t <= 4 and goes(way, t, g):
            part = z_part(b, way, t, g)
            push(part, part, z_ss.at[way, t, g], z_rs.at[way, t, g], step_to[way])

    def share(b, i, g):
        part = part_of(b, g)
        if g == 0:
            for j in (2, 1, 3) if i == 7 else (1, 3):
                push(part, part, x_ss.at[i, j], x_rs.at[i, j], at(x=x_peer[j]))
        push(part, part, s_ss.at[i, 3 + g], s_rs.at[i, 3 + g], sibling)

    def x_near(b, i):
        for j in (1, 3):
            index = base + 2 + x_peer[NX - j]
            part = rows.at[b, index]
            arrive(part, x_ss.at[i, j], x_rs.at[i, j])
            if i < 7:
                half = rows.at[b, index, pl.ds(HB * (j // 2), HB)]
                push(half, half, x_ss.at[i, 2 - 2 * (j // 2)], x_rs.at[i, 2 - 2 * (j // 2)], at(x=x_peer[j]))
            push(part, part, s_ss.at[i, j - 1], s_rs.at[i, j - 1], sibling)

    def x_far(b, i):
        index = base + 2 + x_peer[2]
        part = rows.at[b, index]
        if i < 7:
            for h in (0, 1):
                arrive(rows.at[b, index, pl.ds(HB * h, HB)], x_ss.at[i, 2 - 2 * h], x_rs.at[i, 2 - 2 * h])
        else:
            arrive(part, x_ss.at[i, 2], x_rs.at[i, 2])
        push(part, part, s_ss.at[i, 1], s_rs.at[i, 1], sibling)

    other = (1 - c) * HALF

    def ready(b, i):
        for g in range(3):
            arrive(rows.at[b, other + 2 + x if g == 0 else other + g - 1], s_ss.at[i, 3 + g], s_rs.at[i, 3 + g])
        for j in range(1, NX):
            arrive(rows.at[b, other + 2 + x_peer[NX - j]], s_ss.at[i, j - 1], s_rs.at[i, j - 1])

    def hidden(group):
        gate_act = jnp.zeros((BLK * len(group), UNITS), F32)
        up_act = jnp.zeros((BLK * len(group), UNITS), F32)
        for p in range(PARTS):
            span = slice(p * PW, (p + 1) * PW)
            pieces = [rows[blocks[i], p] for i in group]
            block = pieces[0] if len(pieces) == 1 else jnp.concatenate(pieces, axis=0)
            gate_act += jnp.dot(block, gate[span, :], preferred_element_type=F32)
            up_act += jnp.dot(block, up[span, :], preferred_element_type=F32)
        value = gate_act / (1.0 + jnp.exp(-gate_act)) * up_act
        high = value.astype(BF16)
        low = (value - high.astype(F32)).astype(BF16)
        turned = jnp.dot(high, had[...], preferred_element_type=F32) + jnp.dot(
            low, had[...], preferred_element_type=F32
        )
        for n, i in enumerate(group):
            core_s[blocks[i]] = turned[BLK * n:BLK * n + BLK]

    def core_push(b, i):
        push(core_s.at[b], core_r.at[b], c_ss.at[i], c_rs.at[i], sibling)

    sign = (1 - 2 * c).astype(F32)
    me32 = z * NX + x

    def spread(b, i):
        arrive(core_r.at[b], c_ss.at[i], c_rs.at[i])
        value = (core_r[b] + sign * core_s[b]).astype(BF16)
        for k in range(NX):
            a2a_s[b, k] = value[48 * (k // 2):48 * (k // 2) + 48, 128 * (k % 2):128 * (k % 2) + 128]
        for j in range(NX):
            k = x_peer[j]
            if i == 7 and j == 0:
                a2a_r[me32] = a2a_s[b, k]
            else:
                push(a2a_s.at[b, k], a2a_r.at[me32], a_ss.at[i, j], a_rs.at[0], at(x=k, z=mod(b + 4, NZ)))

    def squeezed(at_col):
        block = ybuf[:, :, at_col:at_col + PW].reshape(NY * TOK, PW)
        return jnp.dot(squeeze, block, preferred_element_type=F32).astype(BF16)

    for g in (0, 1, 2):
        if g < 2:
            span = pl.ds(wide, narrow) if g == 0 else pl.ds(0, wide)
            for i in range(1, NY):
                arrive(ybuf.at[y_peer[NY - i], :, span], y_ss.at[i, g], y_rs.at[i, g])
        if g == 0:
            rows[z, shared] = squeezed(wide)
        else:
            rows[z, base + g - 1] = squeezed((g - 1) * PW)
        for way in (0, 1):
            z_send(z, way, 1, g)
        share(z, 0, g)

    for copy in weights[:2]:
        copy.wait()

    def group(t):
        if t == 0:
            return [0]
        return [2 * t - 1, 2 * t] if t < 4 else [7]

    def work(group):
        for i in group:
            ready(blocks[i], i)
        hidden(group)
        for i in group:
            core_push(blocks[i], i)

    for t in (1, 2, 3, 4):
        for g in (0, 1, 2) if t < 4 else (0, 2, 1):
            for way in (0, 1):
                if not goes(way, t, g):
                    continue
                i = group(t)[way] if t < 4 else 7
                b = blocks[i]
                arrive(z_part(b, way, t, g), z_ss.at[way, t, g], z_rs.at[way, t, g])
                z_send(b, way, t + 1, g)
                if t < 4 or g != 1 or way == 1:
                    share(b, i, g)
            if g == 0:
                for i in group(t - 1):
                    x_near(blocks[i], i)
                if t >= 3:
                    for i in group(t - 3):
                        spread(blocks[i], i)
            if t >= 2 and g == 1:
                work(group(t - 2))
        for i in group(t - 1):
            x_far(blocks[i], i)
    for i in group(2):
        spread(blocks[i], i)
    x_near(blocks[7], 7)
    x_far(blocks[7], 7)
    work(group(3))
    for i in group(3):
        spread(blocks[i], i)
    work([7])
    spread(blocks[7], 7)

    remote(a2a_r.at[pl.ds(0, 31)], a2a_r.at[pl.ds(0, 31)], a_ss.at[0, 0], a_rs.at[0], sibling).wait_recv()
    count = NZ * NX

    def butterfly(values):
        stride = 1
        while stride < len(values):
            for low in range(len(values)):
                if low & stride == 0:
                    upper, lower = values[low], values[low + stride]
                    values[low], values[low + stride] = upper + lower, upper - lower
            stride *= 2
        return values

    for r in range(0, 48, 16):
        for s in range(0, count, 8):
            values = butterfly([a2a_r[s + n, r:r + 16, :].astype(F32) for n in range(8)])
            for n in range(8):
                wide_r[s + n, r:r + 16, :] = values[n]
        for n in range(8):
            values = butterfly([wide_r[n + 8 * q, r:r + 16, :] for q in range(4)])
            for q in range(4):
                back_s[n + 8 * q, r:r + 16, :] = (values[q] * FF ** -0.5).astype(BF16)

    opposite = mod(z + 4, NZ)
    rot[opposite, x] = back_s[me32]
    for dz in (0, 1, 7, 2, 6, 3, 5, 4):
        zz = mod(z + dz, NZ)
        for j in (2, 1, 3, 0):
            if dz + j:
                s = zz * NX + x_peer[j]
                push(back_s.at[s], rot.at[opposite, x], b_ss.at[dz, j], b_rs.at[opposite], at(x=x_peer[j], z=zz))

    weights[2].wait()
    order = [4, 3, 5, 2, 6, 1, 7, 0]
    def down_block(dz, turn):
        b = mod(z + dz, NZ)
        if dz != 4:
            arrive(rot.at[b], b_ss.at[0, 1], b_rs.at[b])
        else:
            arrive(rot.at[b, pl.ds(0, 3)], b_ss.at[0, 1], b_rs.at[b])
        upper = jnp.concatenate([rot[b, 0], rot[b, 1]], axis=1)
        lower = jnp.concatenate([rot[b, 2], rot[b, 3]], axis=1)
        block = jnp.concatenate([upper, lower], axis=0)
        slot = turn % 2
        if turn >= 2:
            remote(sib_s.at[slot], sib_r.at[b], sib_ss.at[slot], sib_rs.at[0], sibling).wait_send()
        for k in range(NX):
            columns = pl.ds(pl.multiple_of((2 * k + 1 - c) * SLICE, 128), SLICE)
            sib_s[slot, k] = jnp.dot(block, down[:, columns], preferred_element_type=F32)
        remote(sib_s.at[slot], sib_r.at[b], sib_ss.at[slot], sib_rs.at[dz], sibling).start()
        for k in range(NX):
            columns = pl.ds(pl.multiple_of((2 * k + c) * SLICE, 128), SLICE)
            own[b, k] = jnp.dot(block, down[:, columns], preferred_element_type=F32)

    def mine(b, k, h):
        half = slice(HB * h, HB * h + HB)
        return own[b, k, half, 0:PW] + sib_r[b, k, half, 0:PW]

    def x_push(dz, n, value, j):
        b = mod(z + dz, NZ)
        xs[b, n] = value.astype(BF16)
        push(xs.at[b, n], xr.at[b, n], x3_ss.at[dz, n], x3_rs.at[dz, n], at(x=x_peer[j]))

    def x_arrive(dz, n):
        arrive(xr.at[mod(z + dz, NZ), n], x3_ss.at[dz, n], x3_rs.at[dz, n])

    def x_scatter(dz):
        b = mod(z + dz, NZ)
        arrive(sib_r.at[b], sib_ss.at[0], sib_rs.at[dz])
        for h, j in ((0, 1), (1, 3)):
            x_push(dz, h, mine(b, x_peer[2], h), j)
        for h, j in ((0, 1), (1, 3)):
            x_push(dz, 2 + h, mine(b, x_peer[j], 1 - h), j)

    def x_relay(dz):
        b = mod(z + dz, NZ)
        for h, j in ((0, 1), (1, 3)):
            x_arrive(dz, h)
            x_push(dz, 4 + h, mine(b, x_peer[j], h) + xr[b, h].astype(F32), j)

    def x_gathered(dz):
        for n in (2, 3, 4, 5):
            x_arrive(dz, n)

    def term(b, part):
        if part:
            pair = (2 * part - 2, 2 * part - 1)
            return jnp.concatenate([own[b, k, :, PW:] + sib_r[b, k, :, PW:] for k in pair], axis=1)
        upper = mine(b, x, 0) + xr[b, 4].astype(F32) + xr[b, 3].astype(F32)
        lower = mine(b, x, 1) + xr[b, 2].astype(F32) + xr[b, 5].astype(F32)
        return jnp.concatenate([upper, lower], axis=0)

    def span_of(way, step, part):
        if step:
            return slice(0, BLK)
        if part:
            return slice(0, BLK) if (part == 1) == (way == 0) else None
        return slice(HB * way, HB * way + HB)

    def z_ref(ref, way, step, part):
        span = span_of(way, step, part)
        return ref.at[way, step, part, pl.ds(span.start, span.stop - span.start)]

    def chain_in(way, step, part):
        arrive(z_ref(zr, way, step, part), z3_ss.at[way, step, part], z3_rs.at[way, step, part])

    def chain(step, parts):
        for part in parts:
            for way in (0, 1):
                span = span_of(way, step, part)
                if span is None:
                    continue
                value = term(mod(z + (4 - step if way == 0 else 4 + step), NZ), part)
                before = span_of(way, step - 1, part) if step else None
                if before is not None:
                    chain_in(way, step - 1, part)
                    came = zr[way, step - 1, part, before, :].astype(F32)
                    pieces = [value[0:before.start], value[before] + came, value[before.stop:BLK]]
                    value = jnp.concatenate([piece for piece in pieces if piece.shape[0]], axis=0)
                zs[way, step, part, span, :] = value[span].astype(BF16)
                push(
                    z_ref(zs, way, step, part), z_ref(zr, way, step, part),
                    z3_ss.at[way, step, part], z3_rs.at[way, step, part], step_to[way],
                )

    down_block(4, 0)
    down_block(3, 1)
    x_scatter(4)
    chain(0, (1, 2))
    down_block(5, 2)
    x_scatter(3)
    x_relay(4)
    down_block(2, 3)
    x_scatter(5)
    x_relay(3)
    x_gathered(4)
    chain(0, (0,))
    chain(1, (1, 2))
    down_block(6, 4)
    x_scatter(2)
    x_relay(5)
    down_block(1, 5)
    x_scatter(6)
    x_relay(2)
    x_gathered(3)
    x_gathered(5)
    chain(1, (0,))
    chain(2, (1, 2))
    down_block(7, 6)
    x_scatter(1)
    x_relay(6)
    down_block(0, 7)
    x_scatter(7)
    x_relay(1)
    x_gathered(2)
    x_gathered(6)
    chain(2, (0,))
    chain(3, (1, 2))
    x_scatter(0)
    x_relay(7)
    x_gathered(1)
    x_gathered(7)
    chain(3, (0,))
    x_relay(0)
    x_gathered(0)

    def final(part):
        return term(z, part) + (zr[0, 3, part].astype(F32) + zr[1, 3, part].astype(F32))

    for part in (1, 2):
        for way in (0, 1):
            chain_in(way, 3, part)
        total = final(part)
        for k in (2 * part - 2, 2 * part - 1):
            columns = slice(ZW * (k % 2), ZW * (k % 2) + ZW)
            fxf[k] = total[:, columns]
            fxs[k] = total[:, columns].astype(BF16)
    for j in (2, 1, 3):
        push(fxs.at[x_peer[j]], fxr.at[j], fx_ss.at[j], fx_rs.at[j], at(x=x_peer[j]))

    def y_send(half, src, dst):
        for i in (2, 1, 3):
            span = pl.ds(pl.multiple_of(y_peer[i] * CAP, 8), CAP)
            push(src.at[span], dst.at[y], y3_ss.at[half, i], y3_rs.at[half, i], at(y=y_peer[i]))
        dst[y] = src[pl.ds(pl.multiple_of(y * CAP, 8), CAP)]

    for way in (0, 1):
        chain_in(way, 3, 0)
    ysa[...] = final(0)
    y_send(0, ysa, yra)

    logits = [column(router_logits[e:e + 1, :]) for e in range(EXPERTS)]
    picked = []
    for ids in (first, second):
        value = logits[0]
        for e in range(1, EXPERTS):
            value = jnp.where(ids == e, logits[e], value)
        picked.append(value)
    share0 = 1.0 / (1.0 + jnp.exp(picked[1] - picked[0]))
    expert, placed = place(CAP)
    combine = jnp.where(placed, jnp.where(first == expert, share0, 1.0 - share0), 0.0)

    total = fxf[x]
    for j in range(1, NX):
        arrive(fxr.at[j], fx_ss.at[j], fx_rs.at[j])
        total += fxr[j].astype(F32)
    ysb[...] = total
    y_send(1, ysb, yrb)
    for half, dst, columns in ((0, yra, slice(0, PW)), (1, yrb, slice(PW, SLICE))):
        for i in range(1, NY):
            arrive(dst.at[y_peer[NY - i]], y3_ss.at[half, i], y3_rs.at[half, i])
        returned = dst[...].reshape(EXPERTS * CAP, columns.stop - columns.start)
        out[:, columns] = jnp.dot(
            combine, returned, precision=lax.Precision.HIGHEST, preferred_element_type=F32
        ).astype(BF16)
    for copy in sent:
        copy.wait_send()
    for slot in (0, 1):
        remote(sib_s.at[slot], sib_r.at[0], sib_ss.at[slot], sib_rs.at[0], sibling).wait_send()


def run(tokens, expert_ids, router_logits, gate_weight, up_weight, down_weight):
    vmem, dma = pltpu.VMEM, pltpu.SemaphoreType.DMA
    scratch = [
        vmem((TOK, D), BF16), vmem((EXPERTS * TOK, 3 * PW), BF16),
        vmem((D, UNITS), BF16), vmem((D, UNITS), BF16), vmem((UNITS, D), BF16),
        vmem((UNITS, UNITS), BF16),
        vmem((NY, TOK, 3 * PW), BF16),
        vmem((NZ, PARTS, BLK, PW), BF16),
        vmem((NZ, BLK, UNITS), F32), vmem((NZ, BLK, UNITS), F32),
        vmem((NZ, NX, 48, 128), BF16),
        vmem((NZ * NX, 48, 128), BF16),
        vmem((NZ * NX, 48, 128), F32), vmem((NZ * NX, 48, 128), BF16),
        vmem((NZ, NX, 48, 128), BF16),
        vmem((NZ, NX, BLK, SLICE), F32),
        vmem((2, NX, BLK, SLICE), F32),
        vmem((NZ, NX, BLK, SLICE), F32),
        vmem((NZ, 6, HB, PW), BF16), vmem((NZ, 6, HB, PW), BF16),
        vmem((2, 4, 3, BLK, PW), BF16), vmem((2, 4, 3, BLK, PW), BF16),
        vmem((NX, BLK, ZW), F32), vmem((NX, BLK, ZW), BF16), vmem((NX, BLK, ZW), BF16),
        vmem((BLK, PW), F32), vmem((BLK, ZW), F32),
        vmem((NY, CAP, PW), F32), vmem((NY, CAP, ZW), F32),
        dma, dma((3,)),
        dma((NY, 2)), dma((NY, 2)),
        dma((2, 5, 3)), dma((2, 5, 3)),
        dma((NZ, NX)), dma((NZ, NX)),
        dma((NZ, 6)), dma((NZ, 6)),
        dma((NZ,)), dma((NZ,)),
        dma((NZ, NX)), dma((1,)),
        dma((NZ, NX)), dma((NZ,)),
        dma((2,)), dma((NZ,)),
        dma((NZ, 6)), dma((NZ, 6)),
        dma((2, 4, 3)), dma((2, 4, 3)),
        dma((NX,)), dma((NX,)),
        dma((2, NY)), dma((2, NY)),
    ]
    return pl.pallas_call(
        kernel,
        out_shape=jax.ShapeDtypeStruct((TOK, SLICE), BF16),
        in_specs=[pl.BlockSpec(memory_space=pl.ANY)]
        + [pl.BlockSpec(memory_space=pltpu.VMEM)] * 2
        + [pl.BlockSpec(memory_space=pl.ANY)] * 3,
        out_specs=pl.BlockSpec(memory_space=pltpu.VMEM),
        scratch_shapes=scratch,
        compiler_params=pltpu.CompilerParams(
            collective_id=1, has_side_effects=True, vmem_limit_bytes=63 * 2 ** 20
        ),
        name="experts",
    )(tokens, expert_ids.T, router_logits.T, gate_weight, up_weight, down_weight)


def solution(mesh):
    placed = (
        P("ed", None),
        P("ed", None),
        P("ed", None),
        P("ed", None, "tp"),
        P("ed", None, "tp"),
        P("ed", "tp", None),
    )
    return jax.shard_map(
        run, mesh=mesh, in_specs=placed, out_specs=P("ed", "tp"), check_vma=False
    )
```

```python
import jax
import jax.numpy as jnp
from jax import lax
from jax.experimental import pallas as pl
from jax.experimental.pallas import tpu as pltpu
from jax.sharding import PartitionSpec as P

MESH = pl.DeviceIdType.MESH
BF16, F32 = jnp.bfloat16, jnp.float32
D = 6144
FF = 16384
EXPERTS = 4
TOK = 32
CAP = 24
NX, NY, NZ = 4, 4, 8
BLK = EXPERTS * CAP
PW = 512
PARTS = D // PW
UNITS = 256
SLICE = 768
HALF = PARTS // 2
HB = BLK // 2
ZW = SLICE - PW


def mod(value, count):
    return lax.rem(value + count, count)


def kernel(
    tokens_hbm, expert_ids, router_logits, gate_hbm, up_hbm, down_hbm, out,
    tokens, packed, gate, up, down, had, ybuf, rows, core_s, core_r, a2a_s, a2a_r, wide_r, back_s, rot,
    own, sib_s, sib_r, xs, xr, zs, zr, fxf, fxs, fxr, ysa, ysb, yra, yrb,
    t_sem, w_sem, y_ss, y_rs, z_ss, z_rs, x_ss, x_rs, s_ss, s_rs, c_ss, c_rs, a_ss, a_rs, b_ss, b_rs,
    sib_ss, sib_rs, x3_ss, x3_rs, z3_ss, z3_rs, fx_ss, fx_rs, y3_ss, y3_rs,
):
    ed, tp = lax.axis_index("ed"), lax.axis_index("tp")
    y, z = lax.div(ed, NZ), lax.rem(ed, NZ)
    x, c = lax.div(tp, 2), lax.rem(tp, 2)

    def at(x=x, y=y, z=z, c=c):
        return (y * NZ + z, x * 2 + c)

    sibling = at(c=1 - c)
    x_peer = [mod(x + i, NX) for i in range(NX)]
    y_peer = [mod(y + i, NY) for i in range(NY)]
    step_to = (at(z=mod(z + 1, NZ)), at(z=mod(z - 1, NZ)))

    def remote(src, dst, send, recv, device):
        return pltpu.make_async_remote_copy(
            src_ref=src, dst_ref=dst, send_sem=send, recv_sem=recv, device_id=device, device_id_type=MESH
        )

    sent = []

    def push(src, dst, send, recv, device):
        copy = remote(src, dst, send, recv, device)
        copy.start()
        sent.append(copy)

    def arrive(dst, send, recv):
        remote(dst, dst, send, recv, sibling).wait_recv()

    tokens_copy = pltpu.make_async_copy(tokens_hbm, tokens, t_sem)
    tokens_copy.start()
    weights = [
        pltpu.make_async_copy(gate_hbm.at[0], gate, w_sem.at[0]),
        pltpu.make_async_copy(up_hbm.at[0], up, w_sem.at[1]),
        pltpu.make_async_copy(down_hbm.at[0], down, w_sem.at[2]),
    ]
    for copy in weights:
        copy.start()

    barrier = pltpu.get_barrier_semaphore()
    greeted = [sibling, *step_to]
    greeted += [at(x=x_peer[i]) for i in range(1, NX)]
    greeted += [at(y=y_peer[i]) for i in range(1, NY)]
    greeted += [at(x=x_peer[i], z=mod(z + dz, NZ)) for dz in (3, 4, 5) for i in range(NX)]
    for device in greeted:
        pl.semaphore_signal(barrier, inc=1, device_id=device, device_id_type=MESH)

    tok_row = lax.broadcasted_iota(jnp.int32, (TOK, TOK), 0)
    tok_col = lax.broadcasted_iota(jnp.int32, (TOK, TOK), 1)
    before = (tok_row > tok_col).astype(F32).astype(BF16)

    def column(values):
        return jnp.sum(jnp.where(tok_row == tok_col, values, jnp.zeros_like(values)), axis=1, keepdims=True)

    first, second = column(expert_ids[0:1, :]), column(expert_ids[1:2, :])

    def place(capacity):
        lane = lax.broadcasted_iota(jnp.int32, (TOK, EXPERTS * capacity), 1)
        expert = jnp.zeros_like(lane)
        for e in range(1, EXPERTS):
            expert += (lane >= e * capacity).astype(jnp.int32)
        chosen = (first == expert) | (second == expert)
        count = jnp.dot(before, chosen.astype(F32).astype(BF16), preferred_element_type=F32)
        return expert, chosen & (count == (lane - expert * capacity).astype(F32))

    _, placing = place(TOK)
    placing = placing.astype(F32).astype(BF16)

    base = c * HALF
    wide, narrow = 2 * PW, PW
    shared = base + 2 + x
    cols_wide = pl.ds(pl.multiple_of(base * PW, 128), wide)
    cols_narrow = pl.ds(pl.multiple_of(shared * PW, 128), narrow)
    tokens_copy.wait()
    kinds = ((0, cols_narrow, pl.ds(wide, narrow)), (1, cols_wide, pl.ds(0, wide)))
    for _, columns, span in kinds:
        packed[:, span] = lax.dot_general(
            placing, tokens[:, columns], (((0,), (0,)), ((), ())), preferred_element_type=F32
        ).astype(BF16)
    pl.semaphore_wait(barrier, len(greeted))
    for kind, _, span in kinds:
        for i in (2, 1, 3):
            slot = pl.ds(pl.multiple_of(y_peer[i] * TOK, TOK), TOK)
            push(packed.at[slot, span], ybuf.at[y, :, span], y_ss.at[i, kind], y_rs.at[i, kind], at(y=y_peer[i]))
    ybuf[y] = packed[pl.ds(pl.multiple_of(y * TOK, TOK), TOK), :]

    both = lax.broadcasted_iota(jnp.int32, (UNITS, UNITS), 0) & lax.broadcasted_iota(jnp.int32, (UNITS, UNITS), 1)
    for shift in (4, 2, 1):
        both = both ^ (both >> shift)
    had[...] = (1 - 2 * (both & 1)).astype(F32).astype(BF16)

    i_row = lax.broadcasted_iota(jnp.int32, (BLK, NY * TOK), 0)
    i_col = lax.broadcasted_iota(jnp.int32, (BLK, NY * TOK), 1)
    squeeze = jnp.zeros((BLK, NY * TOK), F32)
    for s in range(NY):
        inside = (i_row >= CAP * s) & (i_row < CAP * (s + 1)) & (i_col - TOK * s == i_row - CAP * s)
        squeeze = jnp.where(inside, 1.0, squeeze)
    squeeze = squeeze.astype(BF16)

    blocks = [z]
    for t in (1, 2, 3):
        blocks += [mod(z - t, NZ), mod(z + t, NZ)]
    blocks.append(mod(z + 4, NZ))

    def part_of(b, g):
        return rows.at[b, shared if g == 0 else base + g - 1]

    def z_part(b, way, t, g):
        if t == 4 and g == 1:
            return rows.at[b, base, pl.ds(HB * way, HB)]
        return part_of(b, g)

    def goes(way, t, g):
        return t < 4 or g == 1 or (g == 0) == (way == 0)

    def z_send(b, way, t, g):
        if t <= 4 and goes(way, t, g):
            part = z_part(b, way, t, g)
            push(part, part, z_ss.at[way, t, g], z_rs.at[way, t, g], step_to[way])

    def share(b, i, g):
        part = part_of(b, g)
        if g == 0:
            for j in (2, 1, 3) if i == 7 else (1, 3):
                push(part, part, x_ss.at[i, j], x_rs.at[i, j], at(x=x_peer[j]))
        push(part, part, s_ss.at[i, 3 + g], s_rs.at[i, 3 + g], sibling)

    def x_near(b, i):
        for j in (1, 3):
            index = base + 2 + x_peer[NX - j]
            part = rows.at[b, index]
            arrive(part, x_ss.at[i, j], x_rs.at[i, j])
            if i < 7:
                half = rows.at[b, index, pl.ds(HB * (j // 2), HB)]
                push(half, half, x_ss.at[i, 2 - 2 * (j // 2)], x_rs.at[i, 2 - 2 * (j // 2)], at(x=x_peer[j]))
            push(part, part, s_ss.at[i, j - 1], s_rs.at[i, j - 1], sibling)

    def x_far(b, i):
        index = base + 2 + x_peer[2]
        part = rows.at[b, index]
        if i < 7:
            for h in (0, 1):
                arrive(rows.at[b, index, pl.ds(HB * h, HB)], x_ss.at[i, 2 - 2 * h], x_rs.at[i, 2 - 2 * h])
        else:
            arrive(part, x_ss.at[i, 2], x_rs.at[i, 2])
        push(part, part, s_ss.at[i, 1], s_rs.at[i, 1], sibling)

    other = (1 - c) * HALF

    def ready(b, i):
        for g in range(3):
            arrive(rows.at[b, other + 2 + x if g == 0 else other + g - 1], s_ss.at[i, 3 + g], s_rs.at[i, 3 + g])
        for j in range(1, NX):
            arrive(rows.at[b, other + 2 + x_peer[NX - j]], s_ss.at[i, j - 1], s_rs.at[i, j - 1])

    def hidden(group):
        gate_act = jnp.zeros((BLK * len(group), UNITS), F32)
        up_act = jnp.zeros((BLK * len(group), UNITS), F32)
        for p in range(PARTS):
            span = slice(p * PW, (p + 1) * PW)
            pieces = [rows[blocks[i], p] for i in group]
            block = pieces[0] if len(pieces) == 1 else jnp.concatenate(pieces, axis=0)
            gate_act += jnp.dot(block, gate[span, :], preferred_element_type=F32)
            up_act += jnp.dot(block, up[span, :], preferred_element_type=F32)
        value = gate_act / (1.0 + jnp.exp(-gate_act)) * up_act
        high = value.astype(BF16)
        low = (value - high.astype(F32)).astype(BF16)
        turned = jnp.dot(high, had[...], preferred_element_type=F32) + jnp.dot(
            low, had[...], preferred_element_type=F32
        )
        for n, i in enumerate(group):
            core_s[blocks[i]] = turned[BLK * n:BLK * n + BLK]

    def core_push(b, i):
        push(core_s.at[b], core_r.at[b], c_ss.at[i], c_rs.at[i], sibling)

    sign = (1 - 2 * c).astype(F32)
    me32 = z * NX + x

    def spread(b, i):
        arrive(core_r.at[b], c_ss.at[i], c_rs.at[i])
        value = (core_r[b] + sign * core_s[b]).astype(BF16)
        for k in range(NX):
            a2a_s[b, k] = value[48 * (k // 2):48 * (k // 2) + 48, 128 * (k % 2):128 * (k % 2) + 128]
        for j in range(NX):
            k = x_peer[j]
            if i == 7 and j == 0:
                a2a_r[me32] = a2a_s[b, k]
            else:
                push(a2a_s.at[b, k], a2a_r.at[me32], a_ss.at[i, j], a_rs.at[0], at(x=k, z=mod(b + 4, NZ)))

    def squeezed(at_col):
        block = ybuf[:, :, at_col:at_col + PW].reshape(NY * TOK, PW)
        return jnp.dot(squeeze, block, preferred_element_type=F32).astype(BF16)

    for g in (0, 1, 2):
        if g < 2:
            span = pl.ds(wide, narrow) if g == 0 else pl.ds(0, wide)
            for i in range(1, NY):
                arrive(ybuf.at[y_peer[NY - i], :, span], y_ss.at[i, g], y_rs.at[i, g])
        if g == 0:
            rows[z, shared] = squeezed(wide)
        else:
            rows[z, base + g - 1] = squeezed((g - 1) * PW)
        for way in (0, 1):
            z_send(z, way, 1, g)
        share(z, 0, g)

    for copy in weights[:2]:
        copy.wait()

    def group(t):
        if t == 0:
            return [0]
        return [2 * t - 1, 2 * t] if t < 4 else [7]

    def work(group):
        for i in group:
            ready(blocks[i], i)
        hidden(group)
        for i in group:
            core_push(blocks[i], i)

    for t in (1, 2, 3, 4):
        for g in (0, 1, 2) if t < 4 else (0, 2, 1):
            for way in (0, 1):
                if not goes(way, t, g):
                    continue
                i = group(t)[way] if t < 4 else 7
                b = blocks[i]
                arrive(z_part(b, way, t, g), z_ss.at[way, t, g], z_rs.at[way, t, g])
                z_send(b, way, t + 1, g)
                if t < 4 or g != 1 or way == 1:
                    share(b, i, g)
            if g == 0:
                if t >= 2:
                    for i in group(t - 2):
                        x_far(blocks[i], i)
                for i in group(t - 1):
                    x_near(blocks[i], i)
                if t >= 3:
                    for i in group(t - 3):
                        spread(blocks[i], i)
            if t >= 2 and g == 2:
                work(group(t - 2))
    for i in group(3):
        x_far(blocks[i], i)
    for i in group(2):
        spread(blocks[i], i)
    x_near(blocks[7], 7)
    x_far(blocks[7], 7)
    work(group(3))
    for i in group(3):
        spread(blocks[i], i)
    work([7])
    spread(blocks[7], 7)

    remote(a2a_r.at[pl.ds(0, 31)], a2a_r.at[pl.ds(0, 31)], a_ss.at[0, 0], a_rs.at[0], sibling).wait_recv()
    count = NZ * NX

    def butterfly(values):
        stride = 1
        while stride < len(values):
            for low in range(len(values)):
                if low & stride == 0:
                    upper, lower = values[low], values[low + stride]
                    values[low], values[low + stride] = upper + lower, upper - lower
            stride *= 2
        return values

    for r in range(0, 48, 16):
        for s in range(0, count, 8):
            values = butterfly([a2a_r[s + n, r:r + 16, :].astype(F32) for n in range(8)])
            for n in range(8):
                wide_r[s + n, r:r + 16, :] = values[n]
        for n in range(8):
            values = butterfly([wide_r[n + 8 * q, r:r + 16, :] for q in range(4)])
            for q in range(4):
                back_s[n + 8 * q, r:r + 16, :] = (values[q] * FF ** -0.5).astype(BF16)

    opposite = mod(z + 4, NZ)
    rot[opposite, x] = back_s[me32]
    for dz in (0, 1, 7, 2, 6, 3, 5, 4):
        zz = mod(z + dz, NZ)
        for j in (2, 1, 3, 0):
            if dz + j:
                s = zz * NX + x_peer[j]
                push(back_s.at[s], rot.at[opposite, x], b_ss.at[dz, j], b_rs.at[opposite], at(x=x_peer[j], z=zz))

    weights[2].wait()
    order = [4, 3, 5, 2, 6, 1, 7, 0]
    def down_block(dz, turn):
        b = mod(z + dz, NZ)
        if dz != 4:
            arrive(rot.at[b], b_ss.at[0, 1], b_rs.at[b])
        else:
            arrive(rot.at[b, pl.ds(0, 3)], b_ss.at[0, 1], b_rs.at[b])
        upper = jnp.concatenate([rot[b, 0], rot[b, 1]], axis=1)
        lower = jnp.concatenate([rot[b, 2], rot[b, 3]], axis=1)
        block = jnp.concatenate([upper, lower], axis=0)
        slot = turn % 2
        if turn >= 2:
            remote(sib_s.at[slot], sib_r.at[b], sib_ss.at[slot], sib_rs.at[0], sibling).wait_send()
        for k in range(NX):
            columns = pl.ds(pl.multiple_of((2 * k + 1 - c) * SLICE, 128), SLICE)
            sib_s[slot, k] = jnp.dot(block, down[:, columns], preferred_element_type=F32)
        remote(sib_s.at[slot], sib_r.at[b], sib_ss.at[slot], sib_rs.at[dz], sibling).start()
        for k in range(NX):
            columns = pl.ds(pl.multiple_of((2 * k + c) * SLICE, 128), SLICE)
            own[b, k] = jnp.dot(block, down[:, columns], preferred_element_type=F32)

    def mine(b, k, h):
        half = slice(HB * h, HB * h + HB)
        return own[b, k, half, 0:PW] + sib_r[b, k, half, 0:PW]

    def x_push(dz, n, value, j):
        b = mod(z + dz, NZ)
        xs[b, n] = value.astype(BF16)
        push(xs.at[b, n], xr.at[b, n], x3_ss.at[dz, n], x3_rs.at[dz, n], at(x=x_peer[j]))

    def x_arrive(dz, n):
        arrive(xr.at[mod(z + dz, NZ), n], x3_ss.at[dz, n], x3_rs.at[dz, n])

    def x_scatter(dz):
        b = mod(z + dz, NZ)
        arrive(sib_r.at[b], sib_ss.at[0], sib_rs.at[dz])
        for h, j in ((0, 1), (1, 3)):
            x_push(dz, h, mine(b, x_peer[2], h), j)
        for h, j in ((0, 1), (1, 3)):
            x_push(dz, 2 + h, mine(b, x_peer[j], 1 - h), j)

    def x_relay(dz):
        b = mod(z + dz, NZ)
        for h, j in ((0, 1), (1, 3)):
            x_arrive(dz, h)
            x_push(dz, 4 + h, mine(b, x_peer[j], h) + xr[b, h].astype(F32), j)

    def x_gathered(dz):
        for n in (2, 3, 4, 5):
            x_arrive(dz, n)

    def term(b, part):
        if part:
            pair = (2 * part - 2, 2 * part - 1)
            return jnp.concatenate([own[b, k, :, PW:] + sib_r[b, k, :, PW:] for k in pair], axis=1)
        upper = mine(b, x, 0) + xr[b, 4].astype(F32) + xr[b, 3].astype(F32)
        lower = mine(b, x, 1) + xr[b, 2].astype(F32) + xr[b, 5].astype(F32)
        return jnp.concatenate([upper, lower], axis=0)

    def span_of(way, step, part):
        if step:
            return slice(0, BLK)
        if part:
            return slice(0, BLK) if (part == 1) == (way == 0) else None
        return slice(HB * way, HB * way + HB)

    def z_ref(ref, way, step, part):
        span = span_of(way, step, part)
        return ref.at[way, step, part, pl.ds(span.start, span.stop - span.start)]

    def chain_in(way, step, part):
        arrive(z_ref(zr, way, step, part), z3_ss.at[way, step, part], z3_rs.at[way, step, part])

    def chain(step, parts):
        for part in parts:
            for way in (0, 1):
                span = span_of(way, step, part)
                if span is None:
                    continue
                value = term(mod(z + (4 - step if way == 0 else 4 + step), NZ), part)
                before = span_of(way, step - 1, part) if step else None
                if before is not None:
                    chain_in(way, step - 1, part)
                    came = zr[way, step - 1, part, before, :].astype(F32)
                    pieces = [value[0:before.start], value[before] + came, value[before.stop:BLK]]
                    value = jnp.concatenate([piece for piece in pieces if piece.shape[0]], axis=0)
                zs[way, step, part, span, :] = value[span].astype(BF16)
                push(
                    z_ref(zs, way, step, part), z_ref(zr, way, step, part),
                    z3_ss.at[way, step, part], z3_rs.at[way, step, part], step_to[way],
                )

    down_block(4, 0)
    down_block(3, 1)
    x_scatter(4)
    chain(0, (1, 2))
    down_block(5, 2)
    x_scatter(3)
    x_relay(4)
    down_block(2, 3)
    x_scatter(5)
    x_relay(3)
    x_gathered(4)
    chain(0, (0,))
    chain(1, (1, 2))
    down_block(6, 4)
    x_scatter(2)
    x_relay(5)
    down_block(1, 5)
    x_scatter(6)
    x_relay(2)
    x_gathered(3)
    x_gathered(5)
    chain(1, (0,))
    chain(2, (1, 2))
    down_block(7, 6)
    x_scatter(1)
    x_relay(6)
    down_block(0, 7)
    x_scatter(7)
    x_relay(1)
    x_gathered(2)
    x_gathered(6)
    chain(2, (0,))
    chain(3, (1, 2))
    x_scatter(0)
    x_relay(7)
    x_gathered(1)
    x_gathered(7)
    chain(3, (0,))
    x_relay(0)
    x_gathered(0)

    def final(part):
        return term(z, part) + (zr[0, 3, part].astype(F32) + zr[1, 3, part].astype(F32))

    for part in (1, 2):
        for way in (0, 1):
            chain_in(way, 3, part)
        total = final(part)
        for k in (2 * part - 2, 2 * part - 1):
            columns = slice(ZW * (k % 2), ZW * (k % 2) + ZW)
            fxf[k] = total[:, columns]
            fxs[k] = total[:, columns].astype(BF16)
    for j in (2, 1, 3):
        push(fxs.at[x_peer[j]], fxr.at[j], fx_ss.at[j], fx_rs.at[j], at(x=x_peer[j]))

    def y_send(half, src, dst):
        for i in (2, 1, 3):
            span = pl.ds(pl.multiple_of(y_peer[i] * CAP, 8), CAP)
            push(src.at[span], dst.at[y], y3_ss.at[half, i], y3_rs.at[half, i], at(y=y_peer[i]))
        dst[y] = src[pl.ds(pl.multiple_of(y * CAP, 8), CAP)]

    for way in (0, 1):
        chain_in(way, 3, 0)
    ysa[...] = final(0)
    y_send(0, ysa, yra)

    logits = [column(router_logits[e:e + 1, :]) for e in range(EXPERTS)]
    picked = []
    for ids in (first, second):
        value = logits[0]
        for e in range(1, EXPERTS):
            value = jnp.where(ids == e, logits[e], value)
        picked.append(value)
    share0 = 1.0 / (1.0 + jnp.exp(picked[1] - picked[0]))
    expert, placed = place(CAP)
    combine = jnp.where(placed, jnp.where(first == expert, share0, 1.0 - share0), 0.0)

    total = fxf[x]
    for j in range(1, NX):
        arrive(fxr.at[j], fx_ss.at[j], fx_rs.at[j])
        total += fxr[j].astype(F32)
    ysb[...] = total
    y_send(1, ysb, yrb)
    for half, dst, columns in ((0, yra, slice(0, PW)), (1, yrb, slice(PW, SLICE))):
        for i in range(1, NY):
            arrive(dst.at[y_peer[NY - i]], y3_ss.at[half, i], y3_rs.at[half, i])
        returned = dst[...].reshape(EXPERTS * CAP, columns.stop - columns.start)
        out[:, columns] = jnp.dot(
            combine, returned, precision=lax.Precision.HIGHEST, preferred_element_type=F32
        ).astype(BF16)
    for copy in sent:
        copy.wait_send()
    for slot in (0, 1):
        remote(sib_s.at[slot], sib_r.at[0], sib_ss.at[slot], sib_rs.at[0], sibling).wait_send()


def run(tokens, expert_ids, router_logits, gate_weight, up_weight, down_weight):
    vmem, dma = pltpu.VMEM, pltpu.SemaphoreType.DMA
    scratch = [
        vmem((TOK, D), BF16), vmem((EXPERTS * TOK, 3 * PW), BF16),
        vmem((D, UNITS), BF16), vmem((D, UNITS), BF16), vmem((UNITS, D), BF16),
        vmem((UNITS, UNITS), BF16),
        vmem((NY, TOK, 3 * PW), BF16),
        vmem((NZ, PARTS, BLK, PW), BF16),
        vmem((NZ, BLK, UNITS), F32), vmem((NZ, BLK, UNITS), F32),
        vmem((NZ, NX, 48, 128), BF16),
        vmem((NZ * NX, 48, 128), BF16),
        vmem((NZ * NX, 48, 128), F32), vmem((NZ * NX, 48, 128), BF16),
        vmem((NZ, NX, 48, 128), BF16),
        vmem((NZ, NX, BLK, SLICE), F32),
        vmem((2, NX, BLK, SLICE), F32),
        vmem((NZ, NX, BLK, SLICE), F32),
        vmem((NZ, 6, HB, PW), BF16), vmem((NZ, 6, HB, PW), BF16),
        vmem((2, 4, 3, BLK, PW), BF16), vmem((2, 4, 3, BLK, PW), BF16),
        vmem((NX, BLK, ZW), F32), vmem((NX, BLK, ZW), BF16), vmem((NX, BLK, ZW), BF16),
        vmem((BLK, PW), F32), vmem((BLK, ZW), F32),
        vmem((NY, CAP, PW), F32), vmem((NY, CAP, ZW), F32),
        dma, dma((3,)),
        dma((NY, 2)), dma((NY, 2)),
        dma((2, 5, 3)), dma((2, 5, 3)),
        dma((NZ, NX)), dma((NZ, NX)),
        dma((NZ, 6)), dma((NZ, 6)),
        dma((NZ,)), dma((NZ,)),
        dma((NZ, NX)), dma((1,)),
        dma((NZ, NX)), dma((NZ,)),
        dma((2,)), dma((NZ,)),
        dma((NZ, 6)), dma((NZ, 6)),
        dma((2, 4, 3)), dma((2, 4, 3)),
        dma((NX,)), dma((NX,)),
        dma((2, NY)), dma((2, NY)),
    ]
    return pl.pallas_call(
        kernel,
        out_shape=jax.ShapeDtypeStruct((TOK, SLICE), BF16),
        in_specs=[pl.BlockSpec(memory_space=pl.ANY)]
        + [pl.BlockSpec(memory_space=pltpu.VMEM)] * 2
        + [pl.BlockSpec(memory_space=pl.ANY)] * 3,
        out_specs=pl.BlockSpec(memory_space=pltpu.VMEM),
        scratch_shapes=scratch,
        compiler_params=pltpu.CompilerParams(
            collective_id=1, has_side_effects=True, vmem_limit_bytes=63 * 2 ** 20
        ),
        name="experts",
    )(tokens, expert_ids.T, router_logits.T, gate_weight, up_weight, down_weight)


def solution(mesh):
    placed = (
        P("ed", None),
        P("ed", None),
        P("ed", None),
        P("ed", None, "tp"),
        P("ed", None, "tp"),
        P("ed", "tp", None),
    )
    return jax.shard_map(
        run, mesh=mesh, in_specs=placed, out_specs=P("ed", "tp"), check_vma=False
    )
```

```python
import jax
import jax.numpy as jnp
from jax import lax
from jax.experimental import pallas as pl
from jax.experimental.pallas import tpu as pltpu
from jax.sharding import PartitionSpec as P

MESH = pl.DeviceIdType.MESH
BF16, F32 = jnp.bfloat16, jnp.float32
D = 6144
FF = 16384
EXPERTS = 4
TOK = 32
CAP = 24
NX, NY, NZ = 4, 4, 8
BLK = EXPERTS * CAP
PW = 512
PARTS = D // PW
UNITS = 256
SLICE = 768
HALF = PARTS // 2
HB = BLK // 2
ZW = SLICE - PW


def mod(value, count):
    return lax.rem(value + count, count)


def kernel(
    tokens_hbm, expert_ids, router_logits, gate_hbm, up_hbm, down_hbm, out,
    tokens, packed, gate, up, down, had, ybuf, rows, core_s, core_r, a2a_s, a2a_r, wide_r, back_s, rot,
    own, sib_s, sib_r, xs, xr, zs, zr, fxf, fxs, fxr, ysa, ysb, yra, yrb,
    t_sem, w_sem, y_ss, y_rs, z_ss, z_rs, x_ss, x_rs, s_ss, s_rs, c_ss, c_rs, a_ss, a_rs, b_ss, b_rs,
    sib_ss, sib_rs, x3_ss, x3_rs, z3_ss, z3_rs, fx_ss, fx_rs, y3_ss, y3_rs,
):
    ed, tp = lax.axis_index("ed"), lax.axis_index("tp")
    y, z = lax.div(ed, NZ), lax.rem(ed, NZ)
    x, c = lax.div(tp, 2), lax.rem(tp, 2)

    def at(x=x, y=y, z=z, c=c):
        return (y * NZ + z, x * 2 + c)

    sibling = at(c=1 - c)
    x_peer = [mod(x + i, NX) for i in range(NX)]
    y_peer = [mod(y + i, NY) for i in range(NY)]
    step_to = (at(z=mod(z + 1, NZ)), at(z=mod(z - 1, NZ)))

    def remote(src, dst, send, recv, device):
        return pltpu.make_async_remote_copy(
            src_ref=src, dst_ref=dst, send_sem=send, recv_sem=recv, device_id=device, device_id_type=MESH
        )

    sent = []

    def push(src, dst, send, recv, device):
        copy = remote(src, dst, send, recv, device)
        copy.start()
        sent.append(copy)

    def arrive(dst, send, recv):
        remote(dst, dst, send, recv, sibling).wait_recv()

    tokens_copy = pltpu.make_async_copy(tokens_hbm, tokens, t_sem)
    tokens_copy.start()
    weights = [
        pltpu.make_async_copy(gate_hbm.at[0], gate, w_sem.at[0]),
        pltpu.make_async_copy(up_hbm.at[0], up, w_sem.at[1]),
        pltpu.make_async_copy(down_hbm.at[0], down, w_sem.at[2]),
    ]
    for copy in weights:
        copy.start()

    barrier = pltpu.get_barrier_semaphore()
    greeted = [sibling, *step_to]
    greeted += [at(x=x_peer[i]) for i in range(1, NX)]
    greeted += [at(y=y_peer[i]) for i in range(1, NY)]
    greeted += [at(x=x_peer[i], z=mod(z + dz, NZ)) for dz in (3, 4, 5) for i in range(NX)]
    for device in greeted:
        pl.semaphore_signal(barrier, inc=1, device_id=device, device_id_type=MESH)

    tok_row = lax.broadcasted_iota(jnp.int32, (TOK, TOK), 0)
    tok_col = lax.broadcasted_iota(jnp.int32, (TOK, TOK), 1)
    before = (tok_row > tok_col).astype(F32).astype(BF16)

    def column(values):
        return jnp.sum(jnp.where(tok_row == tok_col, values, jnp.zeros_like(values)), axis=1, keepdims=True)

    first, second = column(expert_ids[0:1, :]), column(expert_ids[1:2, :])

    def place(capacity):
        lane = lax.broadcasted_iota(jnp.int32, (TOK, EXPERTS * capacity), 1)
        expert = jnp.zeros_like(lane)
        for e in range(1, EXPERTS):
            expert += (lane >= e * capacity).astype(jnp.int32)
        chosen = (first == expert) | (second == expert)
        count = jnp.dot(before, chosen.astype(F32).astype(BF16), preferred_element_type=F32)
        return expert, chosen & (count == (lane - expert * capacity).astype(F32))

    _, placing = place(TOK)
    placing = placing.astype(F32).astype(BF16)

    base = c * HALF
    wide, narrow = 2 * PW, PW
    shared = base + 2 + x
    cols_wide = pl.ds(pl.multiple_of(base * PW, 128), wide)
    cols_narrow = pl.ds(pl.multiple_of(shared * PW, 128), narrow)
    tokens_copy.wait()
    kinds = ((0, cols_narrow, pl.ds(wide, narrow)), (1, cols_wide, pl.ds(0, wide)))
    for _, columns, span in kinds:
        packed[:, span] = lax.dot_general(
            placing, tokens[:, columns], (((0,), (0,)), ((), ())), preferred_element_type=F32
        ).astype(BF16)
    pl.semaphore_wait(barrier, len(greeted))
    for kind, _, span in kinds:
        for i in (2, 1, 3):
            slot = pl.ds(pl.multiple_of(y_peer[i] * TOK, TOK), TOK)
            push(packed.at[slot, span], ybuf.at[y, :, span], y_ss.at[i, kind], y_rs.at[i, kind], at(y=y_peer[i]))
    ybuf[y] = packed[pl.ds(pl.multiple_of(y * TOK, TOK), TOK), :]

    both = lax.broadcasted_iota(jnp.int32, (UNITS, UNITS), 0) & lax.broadcasted_iota(jnp.int32, (UNITS, UNITS), 1)
    for shift in (4, 2, 1):
        both = both ^ (both >> shift)
    had[...] = (1 - 2 * (both & 1)).astype(F32).astype(BF16)

    i_row = lax.broadcasted_iota(jnp.int32, (BLK, NY * TOK), 0)
    i_col = lax.broadcasted_iota(jnp.int32, (BLK, NY * TOK), 1)
    squeeze = jnp.zeros((BLK, NY * TOK), F32)
    for s in range(NY):
        inside = (i_row >= CAP * s) & (i_row < CAP * (s + 1)) & (i_col - TOK * s == i_row - CAP * s)
        squeeze = jnp.where(inside, 1.0, squeeze)
    squeeze = squeeze.astype(BF16)

    blocks = [z]
    for t in (1, 2, 3):
        blocks += [mod(z - t, NZ), mod(z + t, NZ)]
    blocks.append(mod(z + 4, NZ))

    def part_of(b, g):
        return rows.at[b, shared if g == 0 else base + g - 1]

    def z_part(b, way, t, g):
        if t == 4 and g == 1:
            return rows.at[b, base, pl.ds(HB * way, HB)]
        return part_of(b, g)

    def goes(way, t, g):
        return t < 4 or g == 1 or (g == 0) == (way == 0)

    def z_send(b, way, t, g):
        if t <= 4 and goes(way, t, g):
            part = z_part(b, way, t, g)
            push(part, part, z_ss.at[way, t, g], z_rs.at[way, t, g], step_to[way])

    def share(b, i, g):
        part = part_of(b, g)
        if g == 0:
            for j in (2, 1, 3) if i == 7 else (1, 3):
                push(part, part, x_ss.at[i, j], x_rs.at[i, j], at(x=x_peer[j]))
        push(part, part, s_ss.at[i, 3 + g], s_rs.at[i, 3 + g], sibling)

    def x_near(b, i):
        for j in (1, 3):
            index = base + 2 + x_peer[NX - j]
            part = rows.at[b, index]
            arrive(part, x_ss.at[i, j], x_rs.at[i, j])
            if i < 7:
                half = rows.at[b, index, pl.ds(HB * (j // 2), HB)]
                push(half, half, x_ss.at[i, 2 - 2 * (j // 2)], x_rs.at[i, 2 - 2 * (j // 2)], at(x=x_peer[j]))
            push(part, part, s_ss.at[i, j - 1], s_rs.at[i, j - 1], sibling)

    def x_far(b, i):
        index = base + 2 + x_peer[2]
        part = rows.at[b, index]
        if i < 7:
            for h in (0, 1):
                arrive(rows.at[b, index, pl.ds(HB * h, HB)], x_ss.at[i, 2 - 2 * h], x_rs.at[i, 2 - 2 * h])
        else:
            arrive(part, x_ss.at[i, 2], x_rs.at[i, 2])
        push(part, part, s_ss.at[i, 1], s_rs.at[i, 1], sibling)

    other = (1 - c) * HALF

    def ready(b, i):
        for g in range(3):
            arrive(rows.at[b, other + 2 + x if g == 0 else other + g - 1], s_ss.at[i, 3 + g], s_rs.at[i, 3 + g])
        for j in range(1, NX):
            arrive(rows.at[b, other + 2 + x_peer[NX - j]], s_ss.at[i, j - 1], s_rs.at[i, j - 1])

    def hidden(group):
        gate_act = jnp.zeros((BLK * len(group), UNITS), F32)
        up_act = jnp.zeros((BLK * len(group), UNITS), F32)
        for p in range(PARTS):
            span = slice(p * PW, (p + 1) * PW)
            pieces = [rows[blocks[i], p] for i in group]
            block = pieces[0] if len(pieces) == 1 else jnp.concatenate(pieces, axis=0)
            gate_act += jnp.dot(block, gate[span, :], preferred_element_type=F32)
            up_act += jnp.dot(block, up[span, :], preferred_element_type=F32)
        value = gate_act / (1.0 + jnp.exp(-gate_act)) * up_act
        high = value.astype(BF16)
        low = (value - high.astype(F32)).astype(BF16)
        turned = jnp.dot(high, had[...], preferred_element_type=F32) + jnp.dot(
            low, had[...], preferred_element_type=F32
        )
        for n, i in enumerate(group):
            core_s[blocks[i]] = turned[BLK * n:BLK * n + BLK]

    def core_push(b, i):
        push(core_s.at[b], core_r.at[b], c_ss.at[i], c_rs.at[i], sibling)

    sign = (1 - 2 * c).astype(F32)
    me32 = z * NX + x

    def spread(b, i):
        arrive(core_r.at[b], c_ss.at[i], c_rs.at[i])
        value = (core_r[b] + sign * core_s[b]).astype(BF16)
        for k in range(NX):
            a2a_s[b, k] = value[48 * (k // 2):48 * (k // 2) + 48, 128 * (k % 2):128 * (k % 2) + 128]
        for j in range(NX):
            k = x_peer[j]
            if i == 7 and j == 0:
                a2a_r[me32] = a2a_s[b, k]
            else:
                push(a2a_s.at[b, k], a2a_r.at[me32], a_ss.at[i, j], a_rs.at[0], at(x=k, z=mod(b + 4, NZ)))

    def squeezed(at_col):
        block = ybuf[:, :, at_col:at_col + PW].reshape(NY * TOK, PW)
        return jnp.dot(squeeze, block, preferred_element_type=F32).astype(BF16)

    for g in (0, 1, 2):
        if g < 2:
            span = pl.ds(wide, narrow) if g == 0 else pl.ds(0, wide)
            for i in range(1, NY):
                arrive(ybuf.at[y_peer[NY - i], :, span], y_ss.at[i, g], y_rs.at[i, g])
        if g == 0:
            rows[z, shared] = squeezed(wide)
        else:
            rows[z, base + g - 1] = squeezed((g - 1) * PW)
        for way in (0, 1):
            z_send(z, way, 1, g)
        share(z, 0, g)

    for copy in weights[:2]:
        copy.wait()

    def group(t):
        if t == 0:
            return [0]
        return [2 * t - 1, 2 * t] if t < 4 else [7]

    def work(group):
        for i in group:
            ready(blocks[i], i)
        hidden(group)
        for i in group:
            core_push(blocks[i], i)

    for t in (1, 2, 3, 4):
        for g in (0, 1, 2) if t < 4 else (0, 2, 1):
            for way in (0, 1):
                if not goes(way, t, g):
                    continue
                i = group(t)[way] if t < 4 else 7
                b = blocks[i]
                arrive(z_part(b, way, t, g), z_ss.at[way, t, g], z_rs.at[way, t, g])
                z_send(b, way, t + 1, g)
                if t < 4 or g != 1 or way == 1:
                    share(b, i, g)
            if g == 0:
                if t >= 2:
                    for i in group(t - 2):
                        x_far(blocks[i], i)
                for i in group(t - 1):
                    x_near(blocks[i], i)
                if t >= 3:
                    for i in group(t - 3):
                        spread(blocks[i], i)
            if t >= 2 and g == 2:
                work(group(t - 2))
    for i in group(3):
        x_far(blocks[i], i)
    for i in group(2):
        spread(blocks[i], i)
    x_near(blocks[7], 7)
    x_far(blocks[7], 7)
    work(group(3))
    for i in group(3):
        spread(blocks[i], i)
    work([7])
    spread(blocks[7], 7)

    remote(a2a_r.at[pl.ds(0, 31)], a2a_r.at[pl.ds(0, 31)], a_ss.at[0, 0], a_rs.at[0], sibling).wait_recv()
    count = NZ * NX

    def butterfly(values):
        stride = 1
        while stride < len(values):
            for low in range(len(values)):
                if low & stride == 0:
                    upper, lower = values[low], values[low + stride]
                    values[low], values[low + stride] = upper + lower, upper - lower
            stride *= 2
        return values

    for r in range(0, 48, 16):
        for s in range(0, count, 8):
            values = butterfly([a2a_r[s + n, r:r + 16, :].astype(F32) for n in range(8)])
            for n in range(8):
                wide_r[s + n, r:r + 16, :] = values[n]
        for n in range(8):
            values = butterfly([wide_r[n + 8 * q, r:r + 16, :] for q in range(4)])
            for q in range(4):
                back_s[n + 8 * q, r:r + 16, :] = (values[q] * FF ** -0.5).astype(BF16)

    opposite = mod(z + 4, NZ)
    rot[opposite, x] = back_s[me32]
    for dz in (0, 1, 7, 2, 6, 3, 5, 4):
        zz = mod(z + dz, NZ)
        for j in (2, 1, 3, 0):
            if dz + j:
                s = zz * NX + x_peer[j]
                push(back_s.at[s], rot.at[opposite, x], b_ss.at[dz, j], b_rs.at[opposite], at(x=x_peer[j], z=zz))

    weights[2].wait()
    order = [4, 3, 5, 2, 6, 1, 7, 0]
    def down_block(dz, turn):
        b = mod(z + dz, NZ)
        if dz != 4:
            arrive(rot.at[b], b_ss.at[0, 1], b_rs.at[b])
        else:
            arrive(rot.at[b, pl.ds(0, 3)], b_ss.at[0, 1], b_rs.at[b])
        upper = jnp.concatenate([rot[b, 0], rot[b, 1]], axis=1)
        lower = jnp.concatenate([rot[b, 2], rot[b, 3]], axis=1)
        block = jnp.concatenate([upper, lower], axis=0)
        slot = turn % 2
        if turn >= 2:
            remote(sib_s.at[slot], sib_r.at[b], sib_ss.at[slot], sib_rs.at[0], sibling).wait_send()
        for k in range(NX):
            columns = pl.ds(pl.multiple_of((2 * k + 1 - c) * SLICE, 128), SLICE)
            sib_s[slot, k] = jnp.dot(block, down[:, columns], preferred_element_type=F32)
        remote(sib_s.at[slot], sib_r.at[b], sib_ss.at[slot], sib_rs.at[dz], sibling).start()
        for k in range(NX):
            columns = pl.ds(pl.multiple_of((2 * k + c) * SLICE, 128), SLICE)
            own[b, k] = jnp.dot(block, down[:, columns], preferred_element_type=F32)

    def mine(b, k, h):
        half = slice(HB * h, HB * h + HB)
        return own[b, k, half, 0:PW] + sib_r[b, k, half, 0:PW]

    def x_push(dz, n, value, j):
        b = mod(z + dz, NZ)
        xs[b, n] = value.astype(BF16)
        push(xs.at[b, n], xr.at[b, n], x3_ss.at[dz, n], x3_rs.at[dz, n], at(x=x_peer[j]))

    def x_arrive(dz, n):
        arrive(xr.at[mod(z + dz, NZ), n], x3_ss.at[dz, n], x3_rs.at[dz, n])

    def x_scatter(dz):
        b = mod(z + dz, NZ)
        arrive(sib_r.at[b], sib_ss.at[0], sib_rs.at[dz])
        for h, j in ((0, 1), (1, 3)):
            x_push(dz, h, mine(b, x_peer[2], h), j)
        for h, j in ((0, 1), (1, 3)):
            x_push(dz, 2 + h, mine(b, x_peer[j], 1 - h), j)

    def x_relay(dz):
        b = mod(z + dz, NZ)
        for h, j in ((0, 1), (1, 3)):
            x_arrive(dz, h)
            x_push(dz, 4 + h, mine(b, x_peer[j], h) + xr[b, h].astype(F32), j)

    def x_gathered(dz):
        for n in (2, 3, 4, 5):
            x_arrive(dz, n)

    def term(b, part):
        if part:
            pair = (2 * part - 2, 2 * part - 1)
            return jnp.concatenate([own[b, k, :, PW:] + sib_r[b, k, :, PW:] for k in pair], axis=1)
        upper = mine(b, x, 0) + xr[b, 4].astype(F32) + xr[b, 3].astype(F32)
        lower = mine(b, x, 1) + xr[b, 2].astype(F32) + xr[b, 5].astype(F32)
        return jnp.concatenate([upper, lower], axis=0)

    def span_of(way, step, part):
        if step:
            return slice(0, BLK)
        if part:
            return slice(0, BLK) if (part == 1) == (way == 0) else None
        return slice(HB * way, HB * way + HB)

    def z_ref(ref, way, step, part):
        span = span_of(way, step, part)
        return ref.at[way, step, part, pl.ds(span.start, span.stop - span.start)]

    def chain_in(way, step, part):
        arrive(z_ref(zr, way, step, part), z3_ss.at[way, step, part], z3_rs.at[way, step, part])

    def chain(step, parts):
        for part in parts:
            for way in (0, 1):
                span = span_of(way, step, part)
                if span is None:
                    continue
                value = term(mod(z + (4 - step if way == 0 else 4 + step), NZ), part)
                before = span_of(way, step - 1, part) if step else None
                if before is not None:
                    chain_in(way, step - 1, part)
                    came = zr[way, step - 1, part, before, :].astype(F32)
                    pieces = [value[0:before.start], value[before] + came, value[before.stop:BLK]]
                    value = jnp.concatenate([piece for piece in pieces if piece.shape[0]], axis=0)
                zs[way, step, part, span, :] = value[span].astype(BF16)
                push(
                    z_ref(zs, way, step, part), z_ref(zr, way, step, part),
                    z3_ss.at[way, step, part], z3_rs.at[way, step, part], step_to[way],
                )

    down_block(4, 0)
    down_block(3, 1)
    x_scatter(4)
    chain(0, (1, 2))
    down_block(5, 2)
    x_scatter(3)
    x_relay(4)
    down_block(2, 3)
    x_scatter(5)
    x_relay(3)
    chain(1, (1, 2))
    x_gathered(4)
    chain(0, (0,))
    down_block(6, 4)
    x_scatter(2)
    x_relay(5)
    down_block(1, 5)
    x_scatter(6)
    x_relay(2)
    chain(2, (1, 2))
    x_gathered(3)
    x_gathered(5)
    chain(1, (0,))
    down_block(7, 6)
    x_scatter(1)
    x_relay(6)
    down_block(0, 7)
    x_scatter(7)
    x_relay(1)
    x_gathered(2)
    x_gathered(6)
    chain(2, (0,))
    chain(3, (1, 2))
    x_scatter(0)
    x_relay(7)
    x_gathered(1)
    x_gathered(7)
    chain(3, (0,))
    x_relay(0)
    x_gathered(0)

    def final(part):
        return term(z, part) + (zr[0, 3, part].astype(F32) + zr[1, 3, part].astype(F32))

    for part in (1, 2):
        for way in (0, 1):
            chain_in(way, 3, part)
        total = final(part)
        for k in (2 * part - 2, 2 * part - 1):
            columns = slice(ZW * (k % 2), ZW * (k % 2) + ZW)
            fxf[k] = total[:, columns]
            fxs[k] = total[:, columns].astype(BF16)
    for j in (2, 1, 3):
        push(fxs.at[x_peer[j]], fxr.at[j], fx_ss.at[j], fx_rs.at[j], at(x=x_peer[j]))

    def y_send(half, src, dst):
        for i in (2, 1, 3):
            span = pl.ds(pl.multiple_of(y_peer[i] * CAP, 8), CAP)
            push(src.at[span], dst.at[y], y3_ss.at[half, i], y3_rs.at[half, i], at(y=y_peer[i]))
        dst[y] = src[pl.ds(pl.multiple_of(y * CAP, 8), CAP)]

    for way in (0, 1):
        chain_in(way, 3, 0)
    ysa[...] = final(0)
    y_send(0, ysa, yra)

    logits = [column(router_logits[e:e + 1, :]) for e in range(EXPERTS)]
    picked = []
    for ids in (first, second):
        value = logits[0]
        for e in range(1, EXPERTS):
            value = jnp.where(ids == e, logits[e], value)
        picked.append(value)
    share0 = 1.0 / (1.0 + jnp.exp(picked[1] - picked[0]))
    expert, placed = place(CAP)
    combine = jnp.where(placed, jnp.where(first == expert, share0, 1.0 - share0), 0.0)

    total = fxf[x]
    for j in range(1, NX):
        arrive(fxr.at[j], fx_ss.at[j], fx_rs.at[j])
        total += fxr[j].astype(F32)
    ysb[...] = total
    y_send(1, ysb, yrb)
    for half, dst, columns in ((0, yra, slice(0, PW)), (1, yrb, slice(PW, SLICE))):
        for i in range(1, NY):
            arrive(dst.at[y_peer[NY - i]], y3_ss.at[half, i], y3_rs.at[half, i])
        returned = dst[...].reshape(EXPERTS * CAP, columns.stop - columns.start)
        out[:, columns] = jnp.dot(
            combine, returned, precision=lax.Precision.HIGHEST, preferred_element_type=F32
        ).astype(BF16)
    for copy in sent:
        copy.wait_send()
    for slot in (0, 1):
        remote(sib_s.at[slot], sib_r.at[0], sib_ss.at[slot], sib_rs.at[0], sibling).wait_send()


def run(tokens, expert_ids, router_logits, gate_weight, up_weight, down_weight):
    vmem, dma = pltpu.VMEM, pltpu.SemaphoreType.DMA
    scratch = [
        vmem((TOK, D), BF16), vmem((EXPERTS * TOK, 3 * PW), BF16),
        vmem((D, UNITS), BF16), vmem((D, UNITS), BF16), vmem((UNITS, D), BF16),
        vmem((UNITS, UNITS), BF16),
        vmem((NY, TOK, 3 * PW), BF16),
        vmem((NZ, PARTS, BLK, PW), BF16),
        vmem((NZ, BLK, UNITS), F32), vmem((NZ, BLK, UNITS), F32),
        vmem((NZ, NX, 48, 128), BF16),
        vmem((NZ * NX, 48, 128), BF16),
        vmem((NZ * NX, 48, 128), F32), vmem((NZ * NX, 48, 128), BF16),
        vmem((NZ, NX, 48, 128), BF16),
        vmem((NZ, NX, BLK, SLICE), F32),
        vmem((2, NX, BLK, SLICE), F32),
        vmem((NZ, NX, BLK, SLICE), F32),
        vmem((NZ, 6, HB, PW), BF16), vmem((NZ, 6, HB, PW), BF16),
        vmem((2, 4, 3, BLK, PW), BF16), vmem((2, 4, 3, BLK, PW), BF16),
        vmem((NX, BLK, ZW), F32), vmem((NX, BLK, ZW), BF16), vmem((NX, BLK, ZW), BF16),
        vmem((BLK, PW), F32), vmem((BLK, ZW), F32),
        vmem((NY, CAP, PW), F32), vmem((NY, CAP, ZW), F32),
        dma, dma((3,)),
        dma((NY, 2)), dma((NY, 2)),
        dma((2, 5, 3)), dma((2, 5, 3)),
        dma((NZ, NX)), dma((NZ, NX)),
        dma((NZ, 6)), dma((NZ, 6)),
        dma((NZ,)), dma((NZ,)),
        dma((NZ, NX)), dma((1,)),
        dma((NZ, NX)), dma((NZ,)),
        dma((2,)), dma((NZ,)),
        dma((NZ, 6)), dma((NZ, 6)),
        dma((2, 4, 3)), dma((2, 4, 3)),
        dma((NX,)), dma((NX,)),
        dma((2, NY)), dma((2, NY)),
    ]
    return pl.pallas_call(
        kernel,
        out_shape=jax.ShapeDtypeStruct((TOK, SLICE), BF16),
        in_specs=[pl.BlockSpec(memory_space=pl.ANY)]
        + [pl.BlockSpec(memory_space=pltpu.VMEM)] * 2
        + [pl.BlockSpec(memory_space=pl.ANY)] * 3,
        out_specs=pl.BlockSpec(memory_space=pltpu.VMEM),
        scratch_shapes=scratch,
        compiler_params=pltpu.CompilerParams(
            collective_id=1, has_side_effects=True, vmem_limit_bytes=63 * 2 ** 20
        ),
        name="experts",
    )(tokens, expert_ids.T, router_logits.T, gate_weight, up_weight, down_weight)


def solution(mesh):
    placed = (
        P("ed", None),
        P("ed", None),
        P("ed", None),
        P("ed", None, "tp"),
        P("ed", None, "tp"),
        P("ed", "tp", None),
    )
    return jax.shard_map(
        run, mesh=mesh, in_specs=placed, out_specs=P("ed", "tp"), check_vma=False
    )
```
